32 devices in a mesh: blk: 4 (over y, x), grp: 8 (over z, core).
Axes of the slice: x: 2, y: 2, z: 4, core: 2. Of those that a mesh axis runs over, the one named last changes fastest.
Arguments:
- images: bfloat16 [2048, 1152], P(('blk', 'grp')), may hold values from -6 to 6
- captions: bfloat16 [2048, 1152], P(('blk', 'grp')), may hold values from -6 to 6
- image_head: bfloat16 [1152, 1152], replicated, may hold values from -0.1875 to 0.1875
- text_head: bfloat16 [1152, 1152], replicated, may hold values from -0.1875 to 0.1875
Outputs:
- grad_images: bfloat16 [2048, 1152], P(('blk', 'grp'))
- grad_captions: bfloat16 [2048, 1152], P(('blk', 'grp'))
- grad_image_head: float32 [1152, 1152], P('grp')
- grad_text_head: float32 [1152, 1152], P('grp')
The draws below stay inside these ranges and needn't reach their ends.
All inputs are finite; a program needn't handle non-finite values.
Results may differ from the reference program's by a relative error of at most 0.013.
Values may be sent and summed in bfloat16 or wider, within the bound.
No kernel may reach another device: no remote copies, remote signals or barrier semaphores. Data moves between devices by JAX's collectives and lax.ppermute only.
A program may use at most 128 MiB of HBM per device.

```python
import jax
import jax.numpy as jnp
from jax import lax

D = 1152
BATCH = 2048


def shard_levels(rng, shape, pieces, least, top_value):
    gain = 1.0
    for axis_at, shards_of in pieces:
        draws = jax.random.uniform(jax.random.fold_in(jax.random.fold_in(rng, 6), axis_at), (shards_of,), jnp.float32, least / len(pieces), top_value / len(pieces))
        gain = gain * jnp.repeat(jnp.exp(draws), shape[axis_at] // shards_of).reshape((-1,) + (1,) * (len(shape) - 1 - axis_at))
    return gain


def normal_values(stream_key, dims, scale, reach, shards=(), held_as=jnp.bfloat16):
    drawn = scale * jax.random.normal(stream_key, dims, jnp.float32)
    if shards:
        drawn = drawn * shard_levels(stream_key, dims, shards, -0.22, 0.18)
    return jnp.clip(drawn, -reach, reach).astype(held_as)


def setup_inputs(seed: int = 0) -> dict:
    seeds = jax.random.split(jax.random.key(seed), 5)
    return {
        "images": normal_values(seeds[0], (BATCH, D), 1.0, 6.0, ((0, 32),)),
        "captions": normal_values(seeds[1], (BATCH, D), 1.0, 6.0, ((0, 32),)),
        "image_head": normal_values(seeds[2], (D, D), D ** -0.5, 0.1875),
        "text_head": normal_values(seeds[3], (D, D), D ** -0.5, 0.1875),
    }


logit_scale = 32.0
logit_bias = -3.0
epsilon = 1e-06

def project(features, weight):
    before = jnp.dot(features, weight, preferred_element_type=jnp.float32)
    inverse = lax.rsqrt(lax.optimization_barrier(jnp.sum(before * before, axis=1, keepdims=True)) + epsilon)
    return (before * inverse, inverse)

def unproject(grad_unit, unit, inverse):
    inner_sum = lax.optimization_barrier(jnp.sum(unit * grad_unit, axis=1, keepdims=True))
    return (inverse * (grad_unit - unit * inner_sum)).astype(jnp.bfloat16)

def reference(images, captions, image_head, text_head):
    image_unit, image_inverse = project(images, image_head)
    text_unit, text_inverse = project(captions, text_head)
    image_low = image_unit.astype(jnp.bfloat16)
    text_low = text_unit.astype(jnp.bfloat16)
    logits = logit_scale * lax.dot_general(image_low, text_low, (((1,), (1,)), ((), ())), preferred_element_type=jnp.float32) + logit_bias
    row_ids = lax.broadcasted_iota(jnp.int32, logits.shape, 0)
    col_ids = lax.broadcasted_iota(jnp.int32, logits.shape, 1)
    label_sign = jnp.where(row_ids == col_ids, jnp.float32(1.0), jnp.float32(-1.0))
    pair_weight = (-label_sign * jax.nn.sigmoid(-label_sign * logits)).astype(jnp.bfloat16)
    grad_image_unit = logit_scale * jnp.dot(pair_weight, text_low, preferred_element_type=jnp.float32)
    grad_text_unit = logit_scale * lax.dot_general(pair_weight, image_low, (((0,), (0,)), ((), ())), preferred_element_type=jnp.float32)
    image_back = unproject(grad_image_unit, image_unit, image_inverse)
    text_back = unproject(grad_text_unit, text_unit, text_inverse)
    grad_images = lax.dot_general(image_back, image_head, (((1,), (1,)), ((), ())), preferred_element_type=jnp.float32).astype(jnp.bfloat16)
    grad_captions = lax.dot_general(text_back, text_head, (((1,), (1,)), ((), ())), preferred_element_type=jnp.float32).astype(jnp.bfloat16)
    grad_image_head = lax.dot_general(images, image_back, (((0,), (0,)), ((), ())), preferred_element_type=jnp.float32)
    grad_text_head = lax.dot_general(captions, text_back, (((0,), (0,)), ((), ())), preferred_element_type=jnp.float32)
    return (grad_images, grad_captions, grad_image_head, grad_text_head)
```

```python
import jax
import jax.numpy as jnp
from jax import lax
from jax.sharding import PartitionSpec as P

logit_scale = 32.0
logit_bias = -3.0
epsilon = 1e-06
low = jnp.bfloat16
wide = jnp.float32


def dot(a, b, a_dim, b_dim):
    return lax.dot_general(a, b, (((a_dim,), (b_dim,)), ((), ())), preferred_element_type=wide)


def project(features, weight):
    before = dot(features, weight, 1, 0)
    inverse = lax.rsqrt(jnp.sum(before * before, axis=1, keepdims=True) + epsilon)
    return (before * inverse, inverse)


def unproject(grad_unit, unit, inverse):
    inner_sum = jnp.sum(unit * grad_unit, axis=1, keepdims=True)
    return (inverse * (grad_unit - unit * inner_sum)).astype(low)


def pair_weights(rows_low, cols_low, own):
    logits = logit_scale * dot(rows_low, cols_low, 1, 1) + logit_bias
    if not own:
        return jax.nn.sigmoid(logits).astype(low)
    row_ids = lax.broadcasted_iota(jnp.int32, logits.shape, 0)
    col_ids = lax.broadcasted_iota(jnp.int32, logits.shape, 1)
    label_sign = jnp.where(row_ids == col_ids, wide(1.0), wide(-1.0))
    return (-label_sign * jax.nn.sigmoid(-label_sign * logits)).astype(low)


def per_device(images, captions, image_head, text_head):
    groups = lax.axis_size("blk")
    members = lax.axis_size("grp")
    layers = members // 2
    rows, width = images.shape
    blk_pos = lax.axis_index("blk")
    grp_pos = lax.axis_index("grp")
    layer_pos, core_pos = grp_pos // 2, grp_pos % 2

    def over_blk(array, by):
        return lax.ppermute(array, "blk", [(i, i ^ by) for i in range(groups)])

    def over_layer(array, by):
        return lax.ppermute(array, "grp", [(i, i ^ (2 * by)) for i in range(members)])

    def over_core(array):
        return lax.ppermute(array, "grp", [(i, i ^ 1) for i in range(members)])

    def gather_plane(array):
        mine = jnp.concatenate([array] + [over_blk(array, k) for k in range(1, groups)])
        return jnp.concatenate([mine, over_core(mine)])

    image_blocks = [images] + [over_layer(images, k) for k in range(1, layers)]
    caption_plane = gather_plane(captions)
    image_plane = gather_plane(images)

    share = width // members
    part = -(-share // groups)
    padded = -(-part // 16) * 16
    slot = lax.broadcasted_iota(jnp.int32, (layers * padded, width), 0)
    column = lax.broadcasted_iota(jnp.int32, (layers * padded, width), 1)
    layer = (slot // padded) ^ layer_pos
    within = blk_pos * part + slot % padded
    wanted = (layer * 2 + core_pos) * share + within
    valid = (slot % padded < part) & (within < share)
    choose = ((column == wanted) & valid).astype(low)
    image_columns = dot(choose, image_plane, 1, 1).astype(low)
    caption_columns = dot(choose, caption_plane, 1, 1).astype(low)

    text_unit, text_inverse = project(caption_plane, text_head)
    text_low = text_unit.astype(low)
    weights, image_lows, image_total = [], [], None
    for k in range(layers):
        unit, inverse = project(image_blocks[k], image_head)
        unit_low = unit.astype(low)
        pair_weight = pair_weights(unit_low, text_low, k == 0)
        image_part = dot(pair_weight, text_low, 1, 0)
        if k == 0:
            image_unit, image_inverse = unit, inverse
            image_total = image_part
        else:
            image_total = image_total + over_layer(image_part.astype(low), k).astype(wide)
        weights.append(pair_weight)
        image_lows.append(unit_low)
    text_part = dot(jnp.concatenate(weights), jnp.concatenate(image_lows), 0, 0)
    half = groups * rows
    text_half = text_part[:half] + over_core(text_part[half:].astype(low)).astype(wide)
    text_total = text_half[:rows]
    for k in range(1, groups):
        block = text_half[k * rows : (k + 1) * rows]
        text_total = text_total + over_blk(block.astype(low), k).astype(wide)

    image_back = unproject(logit_scale * image_total, image_unit, image_inverse)
    text_back = unproject(logit_scale * text_total, text_unit[:rows], text_inverse[:rows])
    grad_images = dot(image_back, image_head, 1, 1).astype(low)
    grad_captions = dot(text_back, text_head, 1, 1).astype(low)

    row_of = lax.broadcasted_iota(jnp.int32, (share, groups * padded), 0)
    slot_of = lax.broadcasted_iota(jnp.int32, (share, groups * padded), 1)
    source = (slot_of // padded) ^ blk_pos
    place = ((row_of // part == source) & (row_of % part == slot_of % padded)).astype(low)

    def head_gradient(columns, back):
        terms = dot(columns, gather_plane(back), 1, 0)
        total = terms[:padded]
        for k in range(1, layers):
            block = terms[k * padded : (k + 1) * padded]
            total = total + over_layer(block.astype(low), k).astype(wide)
        total = total.astype(low)
        parts = jnp.concatenate([total] + [over_blk(total, k) for k in range(1, groups)])
        return dot(place, parts, 1, 0)

    grad_image_head = head_gradient(image_columns, image_back)
    grad_text_head = head_gradient(caption_columns, text_back)
    return (grad_images, grad_captions, grad_image_head, grad_text_head)


def solution(mesh):
    return jax.shard_map(
        per_device,
        mesh=mesh,
        in_specs=(P(("blk", "grp"), None), P(("blk", "grp"), None), P(), P()),
        out_specs=(
            P(("blk", "grp"), None),
            P(("blk", "grp"), None),
            P("grp", None),
            P("grp", None),
        ),
        check_vma=False,
    )
```

```python
import functools

import jax
import jax.numpy as jnp
from jax import lax
from jax.experimental import pallas as pl
from jax.experimental.pallas import tpu as pltpu
from jax.sharding import Mesh
from jax.sharding import PartitionSpec as P

logit_scale = 32.0
logit_bias = -3.0
epsilon = 1e-06
low = jnp.bfloat16
wide = jnp.float32


def dot(a, b, a_dim, b_dim):
    return lax.dot_general(a, b, (((a_dim,), (b_dim,)), ((), ())), preferred_element_type=wide)


def project(features, weight):
    before = dot(features, weight, 1, 0)
    inverse = lax.rsqrt(jnp.sum(before * before, axis=1, keepdims=True) + epsilon)
    return (before * inverse, inverse)


def unproject(grad_unit, unit, inverse):
    inner_sum = jnp.sum(unit * grad_unit, axis=1, keepdims=True)
    return (inverse * (grad_unit - unit * inner_sum)).astype(low)


def pair_weights(rows_low, cols_low, own):
    logits = logit_scale * dot(rows_low, cols_low, 1, 1) + logit_bias
    if not own:
        return jax.nn.sigmoid(logits).astype(low)
    row_ids = lax.broadcasted_iota(jnp.int32, logits.shape, 0)
    col_ids = lax.broadcasted_iota(jnp.int32, logits.shape, 1)
    label_sign = jnp.where(row_ids == col_ids, wide(1.0), wide(-1.0))
    return (-label_sign * jax.nn.sigmoid(-label_sign * logits)).astype(low)


def after(array, *others):
    return lax.optimization_barrier((array, *others))[0]


def selectors_kernel(sizes, place_ref, choose_ref, order_ref):
    groups, layers, cores, share, part, padded = sizes
    blk_pos, layer_pos, core_pos = place_ref[0], place_ref[1], place_ref[2]
    width = choose_ref.shape[1]
    row = lax.broadcasted_iota(jnp.int32, (padded, width), 0)
    column = lax.broadcasted_iota(jnp.int32, (padded, width), 1)
    kept = (row < part) & (row < share - blk_pos * part)
    pieces = []
    for core in range(cores):
        for layer in range(layers):
            first = ((layer ^ layer_pos) * cores + (core ^ core_pos)) * share + blk_pos * part
            pieces.append(jnp.where(kept & (column == row + first), wide(1.0), wide(0.0)))
    choose_ref[...] = jnp.concatenate(pieces).astype(low)
    row = lax.broadcasted_iota(jnp.int32, order_ref.shape, 0)
    column = lax.broadcasted_iota(jnp.int32, order_ref.shape, 1)
    found = jnp.zeros(order_ref.shape, wide)
    for k in range(groups):
        at = column - k * padded
        match = (at >= 0) & (at < part) & (row == (k ^ blk_pos) * part + at)
        found = jnp.where(match, wide(1.0), found)
    order_ref[...] = found.astype(low)


def selectors(position, sizes, width):
    groups, layers, cores, share, part, padded = sizes
    return pl.pallas_call(
        functools.partial(selectors_kernel, sizes),
        out_shape=(
            jax.ShapeDtypeStruct((cores * layers * padded, width), low),
            jax.ShapeDtypeStruct((share, groups * padded), low),
        ),
        in_specs=[pl.BlockSpec(memory_space=pltpu.SMEM)],
        out_specs=(pl.BlockSpec(memory_space=pltpu.VMEM),) * 2,
        compiler_params=pltpu.CompilerParams(vmem_limit_bytes=16 * 2**20),
    )(position)


def per_device(images, captions, image_head, text_head):
    groups = lax.axis_size("blk")
    layers = lax.axis_size("layer")
    cores = lax.axis_size("core")
    rows, width = images.shape
    position = jnp.stack([lax.axis_index("blk"), lax.axis_index("layer"), lax.axis_index("core")])

    def over(array, axis, by):
        return lax.ppermute(array, axis, [(i, i ^ by) for i in range(lax.axis_size(axis))])

    def over_blk(array):
        return [array] + [over(array, "blk", k) for k in range(1, groups)]

    def over_core(array):
        return over(array, "core", 1)

    share = width // (layers * cores)
    part = -(-share // groups)
    padded = -(-part // 8) * 8
    sent = layers * padded
    sizes = (groups, layers, cores, share, part, padded)

    caption_blocks = over_blk(captions)
    image_blocks = [images, over(after(images, *caption_blocks), "layer", 1)]
    image_blocks += [over(images, "layer", k) for k in range(2, layers)]
    image_group = [images, over(after(images, image_blocks[-1]), "blk", 1)]
    image_group += [over(after(images, *caption_blocks), "blk", k) for k in range(2, groups)]
    choose, order = selectors(position.astype(jnp.int32), sizes, width)

    text_unit, text_inverse = project(jnp.concatenate(caption_blocks), text_head)
    near_low = text_unit.astype(low)
    text_low = jnp.concatenate([near_low, over_core(near_low)])
    weights, image_lows, image_parts = [None] * layers, [None] * layers, [None] * layers
    for k in (*range(layers - 1, 0, -1), 0):
        unit, inverse = project(image_blocks[k], image_head)
        unit_low = unit.astype(low)
        pair_weight = pair_weights(unit_low, text_low, k == 0)
        image_part = dot(pair_weight, text_low, 1, 0)
        if k == 0:
            image_unit, image_inverse, image_total = unit, inverse, image_part
        else:
            image_parts[k] = over(image_part.astype(low), "layer", k)
        weights[k] = pair_weight
        image_lows[k] = unit_low
    weight, image_low = jnp.concatenate(weights), jnp.concatenate(image_lows)
    half = groups * rows
    far_part = dot(weight[:, half:], image_low, 0, 0).astype(low)
    near_part = dot(weight[:, :half], image_low, 0, 0)
    text_half = near_part + over_core(far_part).astype(wide)
    text_total = text_half[:rows]
    text_out = [text_half[k * rows : (k + 1) * rows].astype(low) for k in range(1, groups)]
    text_out, image_group = lax.optimization_barrier((text_out, image_group))
    text_out[0] = after(text_out[0], image_parts[1])
    text_parts = [over(block, "blk", k + 1) for k, block in enumerate(text_out)]

    image_columns = [dot(choose, after(block, *text_out), 1, 1).astype(low) for block in image_group]
    caption_columns = [dot(choose, after(block, *text_out), 1, 1).astype(low) for block in caption_blocks]
    image_columns, caption_columns = lax.optimization_barrier((image_columns, caption_columns))

    for block in text_parts:
        text_total = text_total + block.astype(wide)
    text_back = unproject(logit_scale * text_total, text_unit[:rows], text_inverse[:rows])
    text_backs = over_blk(text_back)
    for block in image_parts[1:]:
        image_total = image_total + after(block, text_back).astype(wide)
    image_back = unproject(logit_scale * image_total, image_unit, image_inverse)
    image_backs = [image_back] + [None] + [over(image_back, "blk", k) for k in range(2, groups)]
    image_backs[1] = over(after(image_back, *text_backs), "blk", 1)
    grad_images = dot(after(image_back, *image_backs[2:]), image_head, 1, 1).astype(low)
    grad_captions = dot(after(text_back, image_back), text_head, 1, 1).astype(low)

    def head_terms(columns, backs):
        terms = sum(dot(c, b, 1, 0) for c, b in zip(columns, backs))
        terms = terms[:sent] + over_core(terms[sent:].astype(low)).astype(wide)
        out = [terms[k * padded : (k + 1) * padded].astype(low) for k in range(1, layers)]
        return terms[:padded], out

    def over_layers(out):
        return [over(block, "layer", k + 1) for k, block in enumerate(out)]

    def add_up(total, parts):
        for block in parts:
            total = total + block.astype(wide)
        return total.astype(low)

    text_total, text_out = head_terms(caption_columns, text_backs)
    text_parts = over_layers(text_out)
    image_backs = [image_back] + [after(block, *text_out) for block in image_backs[1:]]
    image_total, image_out = head_terms(image_columns, image_backs)
    image_parts = over_layers(image_out)
    text_sum = add_up(text_total, [after(block, *image_out) for block in text_parts])
    text_sums = over_blk(text_sum)
    image_sum = add_up(image_total, [after(block, text_sum) for block in image_parts])
    image_sums = over_blk(image_sum)
    text_sums = [text_sum] + [after(block, image_sum) for block in text_sums[1:]]
    grad_text_head = dot(order, jnp.concatenate(text_sums), 1, 0)
    grad_image_head = dot(order, jnp.concatenate(image_sums), 1, 0)
    return (grad_images, grad_captions, grad_image_head, grad_text_head)


def solution(mesh):
    groups, members = mesh.devices.shape
    fine = Mesh(mesh.devices.reshape(groups, members // 2, 2), ("blk", "layer", "core"))
    pairs, share = P(("blk", "layer", "core"), None), P(("layer", "core"), None)
    return jax.shard_map(
        per_device,
        mesh=fine,
        in_specs=(pairs, pairs, P(), P()),
        out_specs=(pairs, pairs, share, share),
        check_vma=False,
    )
```

```python
import functools
import math

import jax
import jax.numpy as jnp
from jax import lax
from jax.experimental import pallas as pl
from jax.experimental.pallas import tpu as pltpu
from jax.sharding import Mesh
from jax.sharding import PartitionSpec as P

logit_scale = 32.0
logit_bias = -3.0
epsilon = 1e-06
low = jnp.bfloat16
wide = jnp.float32
cost_unit = 1_000_000_000


def dot(a, b, a_dim, b_dim):
    return lax.dot_general(a, b, (((a_dim,), (b_dim,)), ((), ())), preferred_element_type=wide)


def project(features, weight):
    before = dot(features, weight, 1, 0)
    return (before, normalized(before)[0].astype(low))


def normalized(before):
    inverse = lax.rsqrt(jnp.sum(before * before, axis=1, keepdims=True) + epsilon)
    return (before * inverse, inverse)


def call(kernel, outs, *arrays, cost=1, scratch=(), behind=()):
    specs = [pl.BlockSpec(memory_space=pltpu.VMEM)] * len(arrays)
    count = len(arrays)
    shapes = [shape for shape, _ in (*outs, *scratch)] + [array.shape for array in arrays]
    held = sum(math.prod(shape) * 4 for shape in shapes)

    def body(*refs):
        kernel(*refs[:count], *refs[count + len(behind) :])

    return pl.pallas_call(
        body,
        out_shape=tuple(jax.ShapeDtypeStruct(shape, kind) for shape, kind in outs),
        in_specs=specs + [pl.BlockSpec(memory_space=pl.ANY)] * len(behind),
        out_specs=(pl.BlockSpec(memory_space=pltpu.VMEM),) * len(outs),
        scratch_shapes=[pltpu.VMEM(shape, kind) for shape, kind in scratch],
        compiler_params=pltpu.CompilerParams(vmem_limit_bytes=min(48 * 2**20, 4 * 2**20 + held)),
        cost_estimate=pl.CostEstimate(flops=cost * cost_unit, bytes_accessed=cost * cost_unit, transcendentals=0),
    )(*arrays, *behind)


def ready_kernel(shape, image_head_ref, text_head_ref, *refs):
    groups, layers, cores = shape
    image_refs, text_refs, refs = refs[:groups], refs[groups : 2 * groups], refs[2 * groups :]
    image_before_ref, text_before_ref, mine_ref, theirs_ref, turned_ref = refs
    image_before_ref[...] = dot(image_refs[0][...], image_head_ref[...], 1, 0)
    text_before_ref[...] = dot(text_refs[0][...], text_head_ref[...], 1, 0)
    gathered = jnp.concatenate([ref[...].astype(wide) for ref in (*image_refs, *text_refs)])
    turned_ref[...] = gathered.T
    share, layer_pos, core_pos = mine_ref.shape[1], lax.axis_index("layer"), lax.axis_index("core")
    step = math.gcd(share, 8)
    for k in range(layers):
        for ref, core in ((mine_ref, core_pos), (theirs_ref, 1 - core_pos)):
            first = ((k ^ layer_pos) * cores + core) * share
            rows = turned_ref[pl.ds(pl.multiple_of(first // 8 * 8, 8), -(-share // 8) * 8), :]
            for start in range(step, 8, step):
                rows = jnp.where(first % 8 == start, pltpu.roll(rows, rows.shape[0] - start, 0), rows)
            ref[k] = rows[:share].astype(low)


def own_kernel(*refs):
    for k in range(len(refs) // 2):
        refs[len(refs) // 2 + k][...] = refs[k][...]


def text_kernel(image_ref, *refs):
    *in_refs, image_out_ref, low_ref = refs
    rows_kernel(*in_refs, low_ref)
    image_out_ref[...] = image_ref[...]


def rows_kernel(*refs):
    *block_refs, head_ref, low_ref = refs
    low_ref[...] = project(jnp.concatenate([ref[...] for ref in block_refs]), head_ref[...])[1]


def half_kernel(near_ref, far_ref, own_ref, *block_refs):
    total = near_ref[...] + far_ref[...].astype(wide)
    rows = own_ref.shape[0]
    own_ref[...] = total[:rows]
    for k, ref in enumerate(block_refs):
        ref[...] = total[(k + 1) * rows : (k + 2) * rows].astype(ref.dtype)


def back_of(own_ref, before_ref, part_refs):
    total = own_ref[...]
    for ref in part_refs:
        total = total + ref[...].astype(wide)
    unit, inverse = normalized(before_ref[...])
    grad_unit = logit_scale * total
    inner_sum = jnp.sum(unit * grad_unit, axis=1, keepdims=True)
    return (inverse * (grad_unit - unit * inner_sum)).astype(low)


def backs_kernel(layers, groups, *refs):
    image_refs, refs = refs[: layers + 1], refs[layers + 1 :]
    text_refs, refs = refs[: groups + 1], refs[groups + 1 :]
    image_ref, text_ref, *out_refs, all_ref = refs
    width, lanes = image_ref.shape[1], out_refs[0].shape[1]
    image_ref[...] = back_of(*image_refs[:2], image_refs[2:])
    text_ref[...] = back_of(*text_refs[:2], text_refs[2:])
    all_ref[:, :width] = image_ref[...]
    all_ref[:, width : 2 * width] = text_ref[...]
    if all_ref.shape[1] > 2 * width:
        all_ref[:, 2 * width :] = jnp.zeros((all_ref.shape[0], all_ref.shape[1] - 2 * width), low)
    for k, ref in enumerate(out_refs):
        ref[...] = all_ref[:, pl.ds(pl.multiple_of((k ^ lax.axis_index("blk")) * lanes, 128), lanes)]


def grad_kernel(back_ref, head_ref, out_ref):
    out_ref[...] = dot(back_ref[...], head_ref[...], 1, 1).astype(low)


def sum_kernel(own_ref, *refs):
    *part_refs, out_ref = refs
    total = own_ref[...]
    for ref in part_refs:
        total = total + ref[...].astype(wide)
    out_ref[...] = total.astype(low)


def tile_kernel(images_ref, near_ref, far_ref, own_ref, *refs):
    *part_refs, near_part_ref, far_part_ref = refs
    images = images_ref[...]
    rows = own_ref.shape[0]
    near, far = near_ref[...], far_ref[...]
    logits = logit_scale * dot(images, near, 1, 1) + logit_bias
    row = lax.broadcasted_iota(jnp.int32, logits.shape, 0)
    column = lax.broadcasted_iota(jnp.int32, logits.shape, 1)
    sign = jnp.where((row == column) & (row < rows), wide(1.0), wide(-1.0))
    near_weight = (-sign * jax.nn.sigmoid(-sign * logits)).astype(low)
    far_weight = jax.nn.sigmoid(logit_scale * dot(images, far, 1, 1) + logit_bias).astype(low)
    far_part_ref[...] = dot(far_weight, images, 0, 0).astype(low)
    near_part_ref[...] = dot(near_weight, images, 0, 0)
    parts = dot(near_weight, near, 1, 0) + dot(far_weight, far, 1, 0)
    own_ref[...] = parts[:rows]
    for k, ref in enumerate(part_refs):
        ref[...] = parts[(k + 1) * rows : (k + 2) * rows].astype(low)


def terms_kernel(width, turned_ref, *refs):
    *back_refs, out_ref = refs
    backs = jnp.concatenate([ref[...] for ref in back_refs])
    lanes = backs.shape[1]
    of_image = lax.broadcasted_iota(jnp.int32, backs.shape, 1) + lax.axis_index("blk") * lanes < width
    zero = jnp.zeros_like(backs)
    backs = jnp.concatenate([jnp.where(of_image, backs, zero), jnp.where(of_image, zero, backs)])
    for k in range(out_ref.shape[0]):
        out_ref[k] = dot(turned_ref[k], backs, 1, 0).astype(out_ref.dtype)


def token_kernel(out_ref):
    out_ref[...] = jnp.zeros_like(out_ref)


def layers_kernel(cut, mine_ref, theirs_ref, *refs):
    for k in range(mine_ref.shape[0]):
        total = mine_ref[k] + theirs_ref[k].astype(wide)
        refs[2 * k][...] = total[:, :cut].astype(refs[2 * k].dtype)
        refs[2 * k + 1][...] = total[:, cut:].astype(refs[2 * k].dtype)


def heads_kernel(groups, cut, *refs):
    *block_refs, image_ref, text_ref, all_ref = refs
    width, lanes = image_ref.shape[1], all_ref.shape[1] // groups
    for k in range(groups):
        first = pl.multiple_of((k ^ lax.axis_index("blk")) * lanes, 128)
        all_ref[:, pl.ds(first, cut)] = block_refs[k][...].astype(wide)
        all_ref[:, pl.ds(first + cut, lanes - cut)] = block_refs[groups + k][...].astype(wide)
    image_ref[...] = all_ref[:, :width]
    text_ref[...] = all_ref[:, width : 2 * width]


def per_device(images, captions, image_head, text_head):
    groups = lax.axis_size("blk")
    layers = lax.axis_size("layer")
    cores = lax.axis_size("core")
    rows, width = images.shape
    half = groups * rows

    def over(array, axis, by):
        return lax.ppermute(array, axis, [(i, i ^ by) for i in range(lax.axis_size(axis))])

    def over_blk(array):
        return [array] + [over(array, "blk", k) for k in range(1, groups)]

    def over_layers(blocks):
        parts = [over(block, "layer", k) for k, block in reversed(list(enumerate(blocks, 1)))]
        return parts[::-1]

    def over_core(array):
        return over(array, "core", 1)

    share = width // (layers * cores)
    lanes = -(-2 * width // (128 * groups)) * 128
    cut = -(-lanes // 256) * 128
    assert width % 128 == 0 and cores == 2

    block = (rows, width)

    caption_blocks = over_blk(captions)
    image_blocks = over_layers([images] * (layers - 1))
    image_own, text_own = call(own_kernel, [(block, low)] * 2, images, captions, cost=10)
    caption_blocks[0] = text_own
    outs = [(block, low), ((half, width), low)]
    image_own, near_low = call(text_kernel, outs, image_own, *caption_blocks, text_head, cost=2)
    image_group = over_blk(image_own)
    far_low = over_core(near_low)
    image_low = call(
        rows_kernel,
        [((layers * rows, width), low)],
        *(image_own, *image_blocks, image_head),
        behind=(near_low,),
        cost=10,
    )[0]
    outs = [(block, wide)] + [(block, low)] * (layers - 1) + [((half, width), wide), ((half, width), low)]
    image_total, *image_out, near_part, far_part = call(tile_kernel, outs, image_low, near_low, far_low, cost=1, behind=image_group[1:])
    image_parts = [over(block, "layer", k + 1) for k, block in enumerate(image_out)]
    outs = [(block, wide)] + [(block, low)] * (groups - 1)
    text_total, *text_out = call(half_kernel, outs, near_part, over_core(far_part), cost=1)
    text_parts = [over(block, "blk", k + 1) for k, block in enumerate(text_out)]

    turned = ((layers, share, 2 * half), low)
    image_before, text_before, turned_mine, turned_theirs = call(
        functools.partial(ready_kernel, (groups, layers, cores)),
        [(block, wide), (block, wide), turned, turned],
        *(image_head, text_head, *image_group, *caption_blocks),
        scratch=[((width, 2 * half), wide)],
        behind=text_out[:1],
    )
    image_back, text_back, *sends = call(
        functools.partial(backs_kernel, layers, groups),
        [(block, low)] * 2 + [((rows, lanes), low)] * groups,
        *(image_total, image_before, *image_parts, text_total, text_before, *text_parts),
        cost=80,
        scratch=[((rows, groups * lanes), low)],
    )
    backs = [sends[0]] + [over(block, "blk", k + 1) for k, block in enumerate(sends[1:])]
    shape = (layers, share, lanes)
    kernel = functools.partial(terms_kernel, width)
    theirs = call(kernel, [(shape, low)], turned_theirs, *backs)[0]
    mine = call(kernel, [(shape, wide)], turned_mine, *backs, behind=[theirs])[0]
    first, second = (share, cut), (share, lanes - cut)
    outs = [(first, wide), (second, wide)] + [(first, low), (second, low)] * (layers - 1)
    terms = call(functools.partial(layers_kernel, cut), outs, mine, over_core(theirs))
    first_parts, second_parts = (
        [over(part, "layer", k + 1) for k, part in enumerate(terms[i::2])] for i in (2, 3)
    )
    first_sum = call(sum_kernel, [(first, low)], terms[0], *first_parts, cost=50)[0]
    first_sums = over_blk(first_sum)
    second_sum = call(sum_kernel, [(second, low)], terms[1], *second_parts, cost=1)[0]
    token = call(token_kernel, [((8, 128), wide)], behind=first_sums, cost=10)[0]
    blocks = first_sums + over_blk(second_sum)
    grad_images = call(grad_kernel, [(block, low)], image_back, image_head, behind=[second_sum])[0]
    grad_captions = call(grad_kernel, [(block, low)], text_back, text_head, behind=[second_sum])[0]
    grad_image_head, grad_text_head = call(
        functools.partial(heads_kernel, groups, cut),
        [((share, width), wide)] * 2,
        *blocks,
        scratch=[((share, groups * lanes), wide)],
        behind=[token],
    )
    return (grad_images, grad_captions, grad_image_head, grad_text_head)


def solution(mesh):
    groups, members = mesh.devices.shape
    fine = Mesh(mesh.devices.reshape(groups, members // 2, 2), ("blk", "layer", "core"))
    pairs, share = P(("blk", "layer", "core"), None), P(("layer", "core"), None)
    return jax.shard_map(
        per_device,
        mesh=fine,
        in_specs=(pairs, pairs, P(), P()),
        out_specs=(pairs, pairs, share, share),
        check_vma=False,
    )
```

```python
import functools
import math

import jax
import jax.numpy as jnp
from jax import lax
from jax.experimental import pallas as pl
from jax.experimental.pallas import tpu as pltpu
from jax.sharding import Mesh
from jax.sharding import PartitionSpec as P

logit_scale = 32.0
logit_bias = -3.0
epsilon = 1e-06
low = jnp.bfloat16
wide = jnp.float32
cost_unit = 1_000_000_000


def dot(a, b, a_dim, b_dim):
    return lax.dot_general(a, b, (((a_dim,), (b_dim,)), ((), ())), preferred_element_type=wide)


def project(features, weight):
    before = dot(features, weight, 1, 0)
    return (before, normalized(before)[0].astype(low))


def normalized(before):
    inverse = lax.rsqrt(jnp.sum(before * before, axis=1, keepdims=True) + epsilon)
    return (before * inverse, inverse)


def call(kernel, outs, *arrays, cost=1, scratch=(), behind=()):
    specs = [pl.BlockSpec(memory_space=pltpu.VMEM)] * len(arrays)
    count = len(arrays)
    shapes = [shape for shape, _ in (*outs, *scratch)] + [array.shape for array in arrays]
    held = sum(math.prod(shape) * 4 for shape in shapes)

    def body(*refs):
        kernel(*refs[:count], *refs[count + len(behind) :])

    return pl.pallas_call(
        body,
        out_shape=tuple(jax.ShapeDtypeStruct(shape, kind) for shape, kind in outs),
        in_specs=specs + [pl.BlockSpec(memory_space=pl.ANY)] * len(behind),
        out_specs=(pl.BlockSpec(memory_space=pltpu.VMEM),) * len(outs),
        scratch_shapes=[pltpu.VMEM(shape, kind) for shape, kind in scratch],
        compiler_params=pltpu.CompilerParams(vmem_limit_bytes=min(48 * 2**20, 4 * 2**20 + held)),
        cost_estimate=pl.CostEstimate(flops=cost * cost_unit, bytes_accessed=cost * cost_unit, transcendentals=0),
    )(*arrays, *behind)


def ready_kernel(shape, image_head_ref, text_head_ref, *refs):
    groups, layers, cores = shape
    image_refs, text_refs, refs = refs[:groups], refs[groups : 2 * groups], refs[2 * groups :]
    image_before_ref, text_before_ref, mine_ref, theirs_ref, turned_ref = refs
    image_before_ref[...] = dot(image_refs[0][...], image_head_ref[...], 1, 0)
    text_before_ref[...] = dot(text_refs[0][...], text_head_ref[...], 1, 0)
    gathered = jnp.concatenate([ref[...].astype(wide) for ref in (*image_refs, *text_refs)])
    turned_ref[...] = gathered.T
    share, layer_pos, core_pos = mine_ref.shape[1], lax.axis_index("layer"), lax.axis_index("core")
    step = math.gcd(share, 8)
    for k in range(layers):
        for ref, core in ((mine_ref, core_pos), (theirs_ref, 1 - core_pos)):
            first = ((k ^ layer_pos) * cores + core) * share
            rows = turned_ref[pl.ds(pl.multiple_of(first // 8 * 8, 8), -(-share // 8) * 8), :]
            for start in range(step, 8, step):
                rows = jnp.where(first % 8 == start, pltpu.roll(rows, rows.shape[0] - start, 0), rows)
            ref[k] = rows[:share].astype(low)


def own_kernel(*refs):
    for k in range(len(refs) // 2):
        refs[len(refs) // 2 + k][...] = refs[k][...]


def text_kernel(image_ref, *refs):
    *in_refs, image_out_ref, low_ref = refs
    rows_kernel(*in_refs, low_ref)
    image_out_ref[...] = image_ref[...]


def rows_kernel(*refs):
    *block_refs, head_ref, low_ref = refs
    low_ref[...] = project(jnp.concatenate([ref[...] for ref in block_refs]), head_ref[...])[1]


def half_kernel(near_ref, far_ref, own_ref, *block_refs):
    total = near_ref[...] + far_ref[...].astype(wide)
    rows = own_ref.shape[0]
    own_ref[...] = total[:rows]
    for k, ref in enumerate(block_refs):
        ref[...] = total[(k + 1) * rows : (k + 2) * rows].astype(ref.dtype)


def back_of(own_ref, before_ref, part_refs):
    total = own_ref[...]
    for ref in part_refs:
        total = total + ref[...].astype(wide)
    unit, inverse = normalized(before_ref[...])
    grad_unit = logit_scale * total
    inner_sum = jnp.sum(unit * grad_unit, axis=1, keepdims=True)
    return (inverse * (grad_unit - unit * inner_sum)).astype(low)


def backs_kernel(layers, groups, *refs):
    image_refs, refs = refs[: layers + 1], refs[layers + 1 :]
    text_refs, refs = refs[: groups + 1], refs[groups + 1 :]
    image_ref, text_ref, *out_refs, all_ref = refs
    width, lanes = image_ref.shape[1], out_refs[0].shape[1]
    image_ref[...] = back_of(*image_refs[:2], image_refs[2:])
    text_ref[...] = back_of(*text_refs[:2], text_refs[2:])
    all_ref[:, :width] = image_ref[...]
    all_ref[:, width : 2 * width] = text_ref[...]
    if all_ref.shape[1] > 2 * width:
        all_ref[:, 2 * width :] = jnp.zeros((all_ref.shape[0], all_ref.shape[1] - 2 * width), low)
    for k, ref in enumerate(out_refs):
        ref[...] = all_ref[:, pl.ds(pl.multiple_of((k ^ lax.axis_index("blk")) * lanes, 128), lanes)]


def grads_kernel(image_ref, image_head_ref, text_ref, text_head_ref, image_out_ref, text_out_ref, token_ref):
    image_out_ref[...] = dot(image_ref[...], image_head_ref[...], 1, 1).astype(low)
    text_out_ref[...] = dot(text_ref[...], text_head_ref[...], 1, 1).astype(low)
    token_ref[...] = jnp.zeros_like(token_ref)


def sum_kernel(own_ref, *refs):
    *part_refs, out_ref = refs
    total = own_ref[...]
    for ref in part_refs:
        total = total + ref[...].astype(wide)
    out_ref[...] = total.astype(low)


def tile_kernel(images_ref, near_ref, far_ref, own_ref, *refs):
    *part_refs, near_part_ref, far_part_ref = refs
    images = images_ref[...]
    rows = own_ref.shape[0]
    near, far = near_ref[...], far_ref[...]
    logits = logit_scale * dot(images, near, 1, 1) + logit_bias
    row = lax.broadcasted_iota(jnp.int32, logits.shape, 0)
    column = lax.broadcasted_iota(jnp.int32, logits.shape, 1)
    sign = jnp.where((row == column) & (row < rows), wide(1.0), wide(-1.0))
    near_weight = (-sign * jax.nn.sigmoid(-sign * logits)).astype(low)
    far_weight = jax.nn.sigmoid(logit_scale * dot(images, far, 1, 1) + logit_bias).astype(low)
    far_part_ref[...] = dot(far_weight, images, 0, 0).astype(low)
    near_part_ref[...] = dot(near_weight, images, 0, 0)
    parts = dot(near_weight, near, 1, 0) + dot(far_weight, far, 1, 0)
    own_ref[...] = parts[:rows]
    for k, ref in enumerate(part_refs):
        ref[...] = parts[(k + 1) * rows : (k + 2) * rows].astype(low)


def terms_kernel(width, turned_ref, *refs):
    *back_refs, out_ref = refs
    backs = jnp.concatenate([ref[...] for ref in back_refs])
    lanes = backs.shape[1]
    of_image = lax.broadcasted_iota(jnp.int32, backs.shape, 1) + lax.axis_index("blk") * lanes < width
    zero = jnp.zeros_like(backs)
    backs = jnp.concatenate([jnp.where(of_image, backs, zero), jnp.where(of_image, zero, backs)])
    for k in range(out_ref.shape[0]):
        out_ref[k] = dot(turned_ref[k], backs, 1, 0).astype(out_ref.dtype)


def layers_kernel(cut, mine_ref, theirs_ref, *refs):
    for k in range(mine_ref.shape[0]):
        total = mine_ref[k] + theirs_ref[k].astype(wide)
        refs[2 * k][...] = total[:, :cut].astype(refs[2 * k].dtype)
        refs[2 * k + 1][...] = total[:, cut:].astype(refs[2 * k].dtype)


def heads_kernel(groups, cut, *refs):
    *block_refs, image_ref, text_ref, all_ref = refs
    width, lanes = image_ref.shape[1], all_ref.shape[1] // groups
    for k in range(groups):
        first = pl.multiple_of((k ^ lax.axis_index("blk")) * lanes, 128)
        all_ref[:, pl.ds(first, cut)] = block_refs[k][...].astype(wide)
        all_ref[:, pl.ds(first + cut, lanes - cut)] = block_refs[groups + k][...].astype(wide)
    image_ref[...] = all_ref[:, :width]
    text_ref[...] = all_ref[:, width : 2 * width]


def per_device(images, captions, image_head, text_head):
    groups = lax.axis_size("blk")
    layers = lax.axis_size("layer")
    cores = lax.axis_size("core")
    rows, width = images.shape
    half = groups * rows

    def over(array, axis, by):
        return lax.ppermute(array, axis, [(i, i ^ by) for i in range(lax.axis_size(axis))])

    def over_blk(array):
        return [array] + [over(array, "blk", k) for k in range(1, groups)]

    def over_layers(blocks):
        parts = [over(block, "layer", k) for k, block in reversed(list(enumerate(blocks, 1)))]
        return parts[::-1]

    def over_core(array):
        return over(array, "core", 1)

    share = width // (layers * cores)
    lanes = -(-2 * width // (128 * groups)) * 128
    cut = -(-lanes // 256) * 128
    assert width % 128 == 0 and cores == 2

    block = (rows, width)

    caption_blocks = over_blk(captions)
    image_blocks = [over(images, "layer", k) for k in range(1, layers)]
    image_own, text_own = call(own_kernel, [(block, low)] * 2, images, captions, cost=10)
    caption_blocks[0] = text_own
    outs = [(block, low), ((half, width), low)]
    image_own, near_low = call(text_kernel, outs, image_own, *caption_blocks, text_head, cost=2)
    image_group = over_blk(image_own)
    far_low = over_core(near_low)
    image_low = call(
        rows_kernel,
        [((layers * rows, width), low)],
        *(image_own, *image_blocks, image_head),
        behind=(near_low,),
        cost=10,
    )[0]
    outs = [(block, wide)] + [(block, low)] * (layers - 1) + [((half, width), wide), ((half, width), low)]
    image_total, *image_out, near_part, far_part = call(tile_kernel, outs, image_low, near_low, far_low, cost=1)
    image_out[0] = call(own_kernel, [(block, low)], image_out[0], behind=image_group[1:], cost=6)[0]
    image_parts = over_layers(image_out)
    outs = [(block, wide)] + [(block, low)] * (groups - 1)
    text_total, *text_out = call(half_kernel, outs, near_part, over_core(far_part), cost=1)
    text_parts = [over(block, "blk", k + 1) for k, block in enumerate(text_out)]

    turned = ((layers, share, 2 * half), low)
    image_before, text_before, turned_mine, turned_theirs = call(
        functools.partial(ready_kernel, (groups, layers, cores)),
        [(block, wide), (block, wide), turned, turned],
        *(image_head, text_head, *image_group, *caption_blocks),
        scratch=[((width, 2 * half), wide)],
        behind=text_out[:1],
        cost=1,
    )
    image_back, text_back, *sends = call(
        functools.partial(backs_kernel, layers, groups),
        [(block, low)] * 2 + [((rows, lanes), low)] * groups,
        *(image_total, image_before, *image_parts, text_total, text_before, *text_parts),
        cost=80,
        scratch=[((rows, groups * lanes), low)],
    )
    backs = [sends[0]] + [over(block, "blk", k + 1) for k, block in enumerate(sends[1:])]
    shape = (layers, share, lanes)
    kernel = functools.partial(terms_kernel, width)
    theirs = call(kernel, [(shape, low)], turned_theirs, *backs)[0]
    mine = call(kernel, [(shape, wide)], turned_mine, *backs, behind=[theirs])[0]
    first, second = (share, cut), (share, lanes - cut)
    outs = [(first, wide), (second, wide)] + [(first, low), (second, low)] * (layers - 1)
    terms = call(functools.partial(layers_kernel, cut), outs, mine, over_core(theirs))
    first_parts, second_parts = (
        [over(terms[2 * k + i], "layer", k) for k in range(layers - 1, 0, -1)] for i in (0, 1)
    )
    grad_images, grad_captions, token = call(
        grads_kernel,
        [(block, low), (block, low), ((8, 128), wide)],
        *(image_back, image_head, text_back, text_head),
        behind=[first_parts[0]],
    )
    first_sum = call(sum_kernel, [(first, low)], terms[0], *first_parts, cost=50, behind=[token])[0]
    first_sums = over_blk(first_sum)
    second_sum = call(sum_kernel, [(second, low)], terms[1], *second_parts, cost=1)[0]
    last_sum = call(own_kernel, [(second, low)], second_sum, behind=first_sums[1:3], cost=1)[0]
    second_sums = [second_sum] + [over(second_sum, "blk", k) for k in range(1, groups - 1)]
    blocks = first_sums + second_sums + [over(last_sum, "blk", groups - 1)]
    grad_image_head, grad_text_head = call(
        functools.partial(heads_kernel, groups, cut),
        [((share, width), wide)] * 2,
        *blocks,
        scratch=[((share, groups * lanes), wide)],
    )
    return (grad_images, grad_captions, grad_image_head, grad_text_head)


def solution(mesh):
    groups, members = mesh.devices.shape
    fine = Mesh(mesh.devices.reshape(groups, members // 2, 2), ("blk", "layer", "core"))
    pairs, share = P(("blk", "layer", "core"), None), P(("layer", "core"), None)
    return jax.shard_map(
        per_device,
        mesh=fine,
        in_specs=(pairs, pairs, P(), P()),
        out_specs=(pairs, pairs, share, share),
        check_vma=False,
    )
```

```python
import functools
import math

import jax
import jax.numpy as jnp
from jax import lax
from jax.experimental import pallas as pl
from jax.experimental.pallas import tpu as pltpu
from jax.sharding import Mesh
from jax.sharding import PartitionSpec as P

logit_scale = 32.0
logit_bias = -3.0
epsilon = 1e-06
low = jnp.bfloat16
wide = jnp.float32
cost_unit = 1_000_000_000


def dot(a, b, a_dim, b_dim):
    return lax.dot_general(a, b, (((a_dim,), (b_dim,)), ((), ())), preferred_element_type=wide)


def project(features, weight):
    before = dot(features, weight, 1, 0)
    return (before, normalized(before)[0].astype(low))


def normalized(before):
    inverse = lax.rsqrt(jnp.sum(before * before, axis=1, keepdims=True) + epsilon)
    return (before * inverse, inverse)


def call(kernel, outs, *arrays, cost=1, scratch=(), behind=()):
    specs = [pl.BlockSpec(memory_space=pltpu.VMEM)] * len(arrays)
    count = len(arrays)
    shapes = [shape for shape, _ in (*outs, *scratch)] + [array.shape for array in arrays]
    held = sum(math.prod(shape) * 4 for shape in shapes)

    def body(*refs):
        kernel(*refs[:count], *refs[count + len(behind) :])

    return pl.pallas_call(
        body,
        out_shape=tuple(jax.ShapeDtypeStruct(shape, kind) for shape, kind in outs),
        in_specs=specs + [pl.BlockSpec(memory_space=pl.ANY)] * len(behind),
        out_specs=(pl.BlockSpec(memory_space=pltpu.VMEM),) * len(outs),
        scratch_shapes=[pltpu.VMEM(shape, kind) for shape, kind in scratch],
        compiler_params=pltpu.CompilerParams(vmem_limit_bytes=min(48 * 2**20, 4 * 2**20 + held)),
        cost_estimate=pl.CostEstimate(flops=cost * cost_unit, bytes_accessed=cost * cost_unit, transcendentals=0),
    )(*arrays, *behind)


def ready_kernel(shape, image_head_ref, text_head_ref, *refs):
    groups, layers, cores = shape
    image_refs, text_refs, refs = refs[:groups], refs[groups : 2 * groups], refs[2 * groups :]
    image_before_ref, text_before_ref, mine_ref, theirs_ref, turned_ref = refs
    image_before_ref[...] = dot(image_refs[0][...], image_head_ref[...], 1, 0)
    text_before_ref[...] = dot(text_refs[0][...], text_head_ref[...], 1, 0)
    gathered = jnp.concatenate([ref[...].astype(wide) for ref in (*image_refs, *text_refs)])
    turned_ref[...] = gathered.T
    share, layer_pos, core_pos = mine_ref.shape[1], lax.axis_index("layer"), lax.axis_index("core")
    step = math.gcd(share, 8)
    for k in range(layers):
        for ref, core in ((mine_ref, core_pos), (theirs_ref, 1 - core_pos)):
            first = ((k ^ layer_pos) * cores + core) * share
            rows = turned_ref[pl.ds(pl.multiple_of(first // 8 * 8, 8), -(-share // 8) * 8), :]
            for start in range(step, 8, step):
                rows = jnp.where(first % 8 == start, pltpu.roll(rows, rows.shape[0] - start, 0), rows)
            ref[k] = rows[:share].astype(low)


def own_kernel(*refs):
    for k in range(len(refs) // 2):
        refs[len(refs) // 2 + k][...] = refs[k][...]


def text_kernel(image_ref, *refs):
    *in_refs, image_out_ref, low_ref = refs
    rows_kernel(*in_refs, low_ref)
    image_out_ref[...] = image_ref[...]


def rows_kernel(*refs):
    *block_refs, head_ref, low_ref = refs
    low_ref[...] = project(jnp.concatenate([ref[...] for ref in block_refs]), head_ref[...])[1]


def half_kernel(near_ref, far_ref, own_ref, *block_refs):
    total = near_ref[...] + far_ref[...].astype(wide)
    rows = own_ref.shape[0]
    own_ref[...] = total[:rows]
    for k, ref in enumerate(block_refs):
        ref[...] = total[(k + 1) * rows : (k + 2) * rows].astype(ref.dtype)


def back_of(own_ref, before_ref, part_refs):
    total = own_ref[...]
    for ref in part_refs:
        total = total + ref[...].astype(wide)
    unit, inverse = normalized(before_ref[...])
    grad_unit = logit_scale * total
    inner_sum = jnp.sum(unit * grad_unit, axis=1, keepdims=True)
    return (inverse * (grad_unit - unit * inner_sum)).astype(low)


def cuts(chunks, groups, share):
    full, rest = divmod(chunks, groups)
    parts = groups // rest if rest and groups % rest == 0 else 0
    if parts and share % (8 * parts) == 0:
        return full, parts
    return full + (rest > 0), 0


def extra_chunk(cut, groups, blk):
    full, parts = cut
    return groups * full + blk // parts


def backs_kernel(layers, groups, cut, *refs):
    image_refs, refs = refs[: layers + 1], refs[layers + 1 :]
    text_refs, refs = refs[: groups + 1], refs[groups + 1 :]
    image_ref, text_ref, *out_refs, all_ref = refs
    width = image_ref.shape[1]
    image_ref[...] = back_of(*image_refs[:2], image_refs[2:])
    text_ref[...] = back_of(*text_refs[:2], text_refs[2:])
    all_ref[:, :width] = image_ref[...]
    all_ref[:, width : 2 * width] = text_ref[...]
    if all_ref.shape[1] > 2 * width:
        all_ref[:, 2 * width :] = jnp.zeros((all_ref.shape[0], all_ref.shape[1] - 2 * width), low)
    own = cut[0] * 128
    for k, ref in enumerate(out_refs):
        blk = k ^ lax.axis_index("blk")
        ref[:, :own] = all_ref[:, pl.ds(pl.multiple_of(blk * own, 128), own)]
        if cut[1]:
            first = pl.multiple_of(extra_chunk(cut, groups, blk) * 128, 128)
            ref[:, own:] = all_ref[:, pl.ds(first, 128)]


def grads_kernel(image_ref, image_head_ref, text_ref, text_head_ref, image_out_ref, text_out_ref, token_ref):
    image_out_ref[...] = dot(image_ref[...], image_head_ref[...], 1, 1).astype(low)
    text_out_ref[...] = dot(text_ref[...], text_head_ref[...], 1, 1).astype(low)
    token_ref[...] = jnp.zeros_like(token_ref)


def sum_kernel(own_ref, *refs):
    *part_refs, out_ref = refs
    total = own_ref[...]
    for ref in part_refs:
        total = total + ref[...].astype(wide)
    out_ref[...] = total.astype(low)


def tile_kernel(images_ref, near_ref, far_ref, own_ref, *refs):
    *part_refs, near_part_ref, far_part_ref = refs
    images = images_ref[...]
    rows = own_ref.shape[0]
    near, far = near_ref[...], far_ref[...]
    logits = logit_scale * dot(images, near, 1, 1) + logit_bias
    row = lax.broadcasted_iota(jnp.int32, logits.shape, 0)
    column = lax.broadcasted_iota(jnp.int32, logits.shape, 1)
    sign = jnp.where((row == column) & (row < rows), wide(1.0), wide(-1.0))
    near_weight = (-sign * jax.nn.sigmoid(-sign * logits)).astype(low)
    far_weight = jax.nn.sigmoid(logit_scale * dot(images, far, 1, 1) + logit_bias).astype(low)
    far_part_ref[...] = dot(far_weight, images, 0, 0).astype(low)
    near_part_ref[...] = dot(near_weight, images, 0, 0)
    parts = dot(near_weight, near, 1, 0) + dot(far_weight, far, 1, 0)
    own_ref[...] = parts[:rows]
    for k, ref in enumerate(part_refs):
        ref[...] = parts[(k + 1) * rows : (k + 2) * rows].astype(low)


def terms_kernel(width, groups, cut, turned_ref, *refs):
    *back_refs, out_ref = refs
    backs = jnp.concatenate([ref[...] for ref in back_refs])
    blk, own = lax.axis_index("blk"), cut[0] * 128
    lane = lax.broadcasted_iota(jnp.int32, backs.shape, 1)
    column = lane + blk * own
    if cut[1]:
        column = jnp.where(lane < own, column, lane - own + extra_chunk(cut, groups, blk) * 128)
    of_image = column < width
    zero = jnp.zeros_like(backs)
    backs = jnp.concatenate([jnp.where(of_image, backs, zero), jnp.where(of_image, zero, backs)])
    for k in range(out_ref.shape[0]):
        out_ref[k] = dot(turned_ref[k], backs, 1, 0).astype(out_ref.dtype)


def layers_kernel(cut, mine_ref, theirs_ref, *refs):
    own, parts = cut[0] * 128, cut[1]
    lanes = refs[0].shape[1]
    for k in range(mine_ref.shape[0]):
        total = mine_ref[k] + theirs_ref[k].astype(wide)
        second = total[:, lanes:own]
        if parts:
            part = total.shape[0] // parts
            extra = total[:part, own:]
            for i in range(1, parts):
                mine = lax.axis_index("blk") % parts == i
                extra = jnp.where(mine, total[i * part : (i + 1) * part, own:], extra)
            second = jnp.concatenate([second, extra])
        refs[2 * k][...] = total[:, :lanes].astype(refs[2 * k].dtype)
        refs[2 * k + 1][...] = second.astype(refs[2 * k].dtype)


def heads_kernel(groups, cut, *refs):
    *block_refs, image_ref, text_ref, all_ref = refs
    (share, width), (_, lanes), (own, parts) = image_ref.shape, block_refs[0].shape, (cut[0] * 128, cut[1])
    for k in range(groups):
        blk = k ^ lax.axis_index("blk")
        first = pl.multiple_of(blk * own, 128)
        second = block_refs[groups + k][...].astype(wide)
        all_ref[:, pl.ds(first, lanes)] = block_refs[k][...].astype(wide)
        all_ref[:, pl.ds(first + lanes, own - lanes)] = second[:share]
        if parts:
            part = share // parts
            row = pl.multiple_of(blk % parts * part, 8)
            column = pl.multiple_of(extra_chunk(cut, groups, blk) * 128, 128)
            all_ref[pl.ds(row, part), pl.ds(column, 128)] = second[share:]
    image_ref[...] = all_ref[:, :width]
    text_ref[...] = all_ref[:, width : 2 * width]


def per_device(images, captions, image_head, text_head):
    groups = lax.axis_size("blk")
    layers = lax.axis_size("layer")
    cores = lax.axis_size("core")
    rows, width = images.shape
    half = groups * rows

    def over(array, axis, by):
        return lax.ppermute(array, axis, [(i, i ^ by) for i in range(lax.axis_size(axis))])

    def over_blk(array):
        return [array] + [over(array, "blk", k) for k in range(1, groups)]

    def over_layers(blocks):
        parts = [over(block, "layer", k) for k, block in reversed(list(enumerate(blocks, 1)))]
        return parts[::-1]

    def over_core(array):
        return over(array, "core", 1)

    share = width // (layers * cores)
    cut = cuts(2 * width // 128, groups, share)
    own, parts = cut[0] * 128, cut[1]
    lanes = own + 128 * (parts > 0)
    columns = max(groups * own, 2 * width)
    first = (share, own - 128 if parts else -(-own // 256) * 128)
    second = (share + share // parts, 128) if parts else (share, own - first[1])
    assert width % 128 == 0 and cores == 2

    block = (rows, width)

    caption_blocks = over_blk(captions)
    image_blocks = [over(images, "layer", k) for k in range(1, layers)]
    image_own, text_own = call(own_kernel, [(block, low)] * 2, images, captions, cost=10)
    caption_blocks[0] = text_own
    outs = [(block, low), ((half, width), low)]
    image_own, near_low = call(text_kernel, outs, image_own, *caption_blocks, text_head, cost=2)
    image_group = over_blk(image_own)
    far_low = over_core(near_low)
    image_low = call(
        rows_kernel,
        [((layers * rows, width), low)],
        *(image_own, *image_blocks, image_head),
        behind=(near_low,),
        cost=10,
    )[0]
    outs = [(block, wide)] + [(block, low)] * (layers - 1) + [((half, width), wide), ((half, width), low)]
    image_total, *image_out, near_part, far_part = call(tile_kernel, outs, image_low, near_low, far_low, cost=1)
    image_out[0] = call(own_kernel, [(block, low)], image_out[0], behind=image_group[1:], cost=6)[0]
    image_parts = over_layers(image_out)
    outs = [(block, wide)] + [(block, low)] * (groups - 1)
    text_total, *text_out = call(half_kernel, outs, near_part, over_core(far_part), cost=1)
    text_parts = [over(block, "blk", k + 1) for k, block in enumerate(text_out)]

    turned = ((layers, share, 2 * half), low)
    image_before, text_before, turned_mine, turned_theirs = call(
        functools.partial(ready_kernel, (groups, layers, cores)),
        [(block, wide), (block, wide), turned, turned],
        *(image_head, text_head, *image_group, *caption_blocks),
        scratch=[((width, 2 * half), wide)],
        behind=text_out[:1],
        cost=1,
    )
    image_back, text_back, *sends = call(
        functools.partial(backs_kernel, layers, groups, cut),
        [(block, low)] * 2 + [((rows, lanes), low)] * groups,
        *(image_total, image_before, *image_parts, text_total, text_before, *text_parts),
        cost=80,
        scratch=[((rows, columns), low)],
    )
    backs = [sends[0]] + [over(block, "blk", k + 1) for k, block in enumerate(sends[1:])]
    shape = (layers, share, lanes)
    kernel = functools.partial(terms_kernel, width, groups, cut)
    theirs = call(kernel, [(shape, low)], turned_theirs, *backs)[0]
    mine = call(kernel, [(shape, wide)], turned_mine, *backs, behind=[theirs])[0]
    outs = [(first, wide), (second, wide)] + [(first, low), (second, low)] * (layers - 1)
    terms = call(functools.partial(layers_kernel, cut), outs, mine, over_core(theirs))
    first_parts, second_parts = (
        [over(terms[2 * k + i], "layer", k) for k in range(layers - 1, 0, -1)] for i in (0, 1)
    )
    grad_images, grad_captions, token = call(
        grads_kernel,
        [(block, low), (block, low), ((8, 128), wide)],
        *(image_back, image_head, text_back, text_head),
        behind=[first_parts[0]],
    )
    first_sum = call(sum_kernel, [(first, low)], terms[0], *first_parts, cost=50, behind=[token])[0]
    first_sums = over_blk(first_sum)
    second_sum = call(sum_kernel, [(second, low)], terms[1], *second_parts, cost=1)[0]
    last_sum = call(own_kernel, [(second, low)], second_sum, behind=first_sums[1:3], cost=1)[0]
    second_sums = [second_sum] + [over(second_sum, "blk", k) for k in range(1, groups - 1)]
    blocks = first_sums + second_sums + [over(last_sum, "blk", groups - 1)]
    grad_image_head, grad_text_head = call(
        functools.partial(heads_kernel, groups, cut),
        [((share, width), wide)] * 2,
        *blocks,
        scratch=[((share, columns), wide)],
    )
    return (grad_images, grad_captions, grad_image_head, grad_text_head)


def solution(mesh):
    groups, members = mesh.devices.shape
    fine = Mesh(mesh.devices.reshape(groups, members // 2, 2), ("blk", "layer", "core"))
    pairs, share = P(("blk", "layer", "core"), None), P(("layer", "core"), None)
    return jax.shard_map(
        per_device,
        mesh=fine,
        in_specs=(pairs, pairs, P(), P()),
        out_specs=(pairs, pairs, share, share),
        check_vma=False,
    )
```

```python
import functools
import math

import jax
import jax.numpy as jnp
from jax import lax
from jax.experimental import pallas as pl
from jax.experimental.pallas import tpu as pltpu
from jax.sharding import Mesh
from jax.sharding import PartitionSpec as P

logit_scale = 32.0
logit_bias = -3.0
epsilon = 1e-06
low = jnp.bfloat16
near = 2
wide = jnp.float32
cost_unit = 1_000_000_000


def dot(a, b, a_dim, b_dim):
    return lax.dot_general(a, b, (((a_dim,), (b_dim,)), ((), ())), preferred_element_type=wide)


def project(features, weight):
    before = dot(features, weight, 1, 0)
    return (before, normalized(before)[0].astype(low))


def normalized(before):
    inverse = lax.rsqrt(jnp.sum(before * before, axis=1, keepdims=True) + epsilon)
    return (before * inverse, inverse)


def call(kernel, outs, *arrays, cost=1, scratch=(), behind=()):
    specs = [pl.BlockSpec(memory_space=pltpu.VMEM)] * len(arrays)
    count = len(arrays)
    shapes = [shape for shape, _ in (*outs, *scratch)] + [array.shape for array in arrays]
    held = sum(math.prod(shape) * 4 for shape in shapes)

    def body(*refs):
        kernel(*refs[:count], *refs[count + len(behind) :])

    return pl.pallas_call(
        body,
        out_shape=tuple(jax.ShapeDtypeStruct(shape, kind) for shape, kind in outs),
        in_specs=specs + [pl.BlockSpec(memory_space=pl.ANY)] * len(behind),
        out_specs=(pl.BlockSpec(memory_space=pltpu.VMEM),) * len(outs),
        scratch_shapes=[pltpu.VMEM(shape, kind) for shape, kind in scratch],
        compiler_params=pltpu.CompilerParams(vmem_limit_bytes=min(48 * 2**20, 4 * 2**20 + held)),
        cost_estimate=pl.CostEstimate(flops=cost * cost_unit, bytes_accessed=cost * cost_unit, transcendentals=0),
    )(*arrays, *behind)


def ready_kernel(shape, image_head_ref, text_head_ref, *refs):
    groups, layers, cores = shape
    image_refs, text_refs, refs = refs[:groups], refs[groups : 2 * groups], refs[2 * groups :]
    image_before_ref, text_before_ref, *out_refs, turned_ref = refs
    image_before_ref[...] = dot(image_refs[0][...], image_head_ref[...], 1, 0)
    text_before_ref[...] = dot(text_refs[0][...], text_head_ref[...], 1, 0)
    gathered = jnp.concatenate([ref[...].astype(wide) for ref in (*image_refs, *text_refs)])
    turned_ref[...] = gathered.T
    share, layer_pos, core_pos = out_refs[0].shape[1], lax.axis_index("layer"), lax.axis_index("core")
    step = math.gcd(share, 8)
    for k in range(layers):
        for i, core in enumerate((core_pos, 1 - core_pos)):
            first = ((k ^ layer_pos) * cores + core) * share
            rows = turned_ref[pl.ds(pl.multiple_of(first // 8 * 8, 8), -(-share // 8) * 8), :]
            for start in range(step, 8, step):
                rows = jnp.where(first % 8 == start, pltpu.roll(rows, rows.shape[0] - start, 0), rows)
            out_refs[2 * i + (k >= near)][k - near * (k >= near)] = rows[:share].astype(low)


def own_kernel(*refs):
    for k in range(len(refs) // 2):
        refs[len(refs) // 2 + k][...] = refs[k][...]


def text_kernel(image_ref, *refs):
    *in_refs, image_out_ref, low_ref = refs
    rows_kernel(*in_refs, low_ref)
    image_out_ref[...] = image_ref[...]


def rows_kernel(*refs):
    *block_refs, head_ref, low_ref = refs
    low_ref[...] = project(jnp.concatenate([ref[...] for ref in block_refs]), head_ref[...])[1]


def token_kernel(out_ref):
    out_ref[...] = jnp.zeros_like(out_ref)


def half_kernel(near_ref, far_ref, own_ref, *block_refs):
    total = near_ref[...] + far_ref[...].astype(wide)
    rows = own_ref.shape[0]
    own_ref[...] = total[:rows]
    for k, ref in enumerate(block_refs):
        ref[...] = total[(k + 1) * rows : (k + 2) * rows].astype(ref.dtype)


def back_of(own_ref, before_ref, part_refs):
    total = own_ref[...]
    for ref in part_refs:
        total = total + ref[...].astype(wide)
    unit, inverse = normalized(before_ref[...])
    grad_unit = logit_scale * total
    inner_sum = jnp.sum(unit * grad_unit, axis=1, keepdims=True)
    return (inverse * (grad_unit - unit * inner_sum)).astype(low)


def cuts(chunks, groups, share):
    full, rest = divmod(chunks, groups)
    parts = groups // rest if rest and groups % rest == 0 else 0
    if parts and share % (8 * parts) == 0:
        return full, parts
    return full + (rest > 0), 0


def extra_chunk(cut, groups, blk):
    full, parts = cut
    return groups * full + blk // parts


def backs_kernel(layers, groups, cut, *refs):
    image_refs, refs = refs[: layers + 1], refs[layers + 1 :]
    text_refs, refs = refs[: groups + 1], refs[groups + 1 :]
    image_ref, text_ref, *out_refs, all_ref = refs
    width = image_ref.shape[1]
    image_ref[...] = back_of(*image_refs[:2], image_refs[2:])
    text_ref[...] = back_of(*text_refs[:2], text_refs[2:])
    all_ref[:, :width] = image_ref[...]
    all_ref[:, width : 2 * width] = text_ref[...]
    if all_ref.shape[1] > 2 * width:
        all_ref[:, 2 * width :] = jnp.zeros((all_ref.shape[0], all_ref.shape[1] - 2 * width), low)
    own = cut[0] * 128
    for k, ref in enumerate(out_refs):
        blk = k ^ lax.axis_index("blk")
        ref[:, :own] = all_ref[:, pl.ds(pl.multiple_of(blk * own, 128), own)]
        if cut[1]:
            first = pl.multiple_of(extra_chunk(cut, groups, blk) * 128, 128)
            ref[:, own:] = all_ref[:, pl.ds(first, 128)]


def grads_kernel(image_ref, image_head_ref, text_ref, text_head_ref, image_out_ref, text_out_ref, token_ref):
    image_out_ref[...] = dot(image_ref[...], image_head_ref[...], 1, 1).astype(low)
    text_out_ref[...] = dot(text_ref[...], text_head_ref[...], 1, 1).astype(low)
    token_ref[...] = jnp.zeros_like(token_ref)


def add_kernel(*refs):
    *part_refs, out_ref = refs
    total = part_refs[0][...].astype(wide)
    for ref in part_refs[1:]:
        total = total + ref[...].astype(wide)
    out_ref[...] = total


def sum_kernel(own_ref, *refs):
    *part_refs, out_ref = refs
    total = own_ref[...]
    for ref in part_refs:
        total = total + ref[...].astype(wide)
    out_ref[...] = total.astype(low)


def tile_kernel(images_ref, near_ref, far_ref, own_ref, *refs):
    *part_refs, near_part_ref, far_part_ref = refs
    images = images_ref[...]
    rows = own_ref.shape[0]
    near, far = near_ref[...], far_ref[...]
    logits = logit_scale * dot(images, near, 1, 1) + logit_bias
    row = lax.broadcasted_iota(jnp.int32, logits.shape, 0)
    column = lax.broadcasted_iota(jnp.int32, logits.shape, 1)
    sign = jnp.where((row == column) & (row < rows), wide(1.0), wide(-1.0))
    near_weight = (-sign * jax.nn.sigmoid(-sign * logits)).astype(low)
    far_weight = jax.nn.sigmoid(logit_scale * dot(images, far, 1, 1) + logit_bias).astype(low)
    far_part_ref[...] = dot(far_weight, images, 0, 0).astype(low)
    near_part_ref[...] = dot(near_weight, images, 0, 0)
    parts = dot(near_weight, near, 1, 0) + dot(far_weight, far, 1, 0)
    own_ref[...] = parts[:rows]
    for k, ref in enumerate(part_refs):
        ref[...] = parts[(k + 1) * rows : (k + 2) * rows].astype(low)


def terms_kernel(width, groups, cut, turned_ref, *refs):
    *back_refs, out_ref = refs
    backs = jnp.concatenate([ref[...] for ref in back_refs[:1] + back_refs[:0:-1]])
    blk, own = lax.axis_index("blk"), cut[0] * 128
    lane = lax.broadcasted_iota(jnp.int32, backs.shape, 1)
    column = lane + blk * own
    if cut[1]:
        column = jnp.where(lane < own, column, lane - own + extra_chunk(cut, groups, blk) * 128)
    of_image = column < width
    zero = jnp.zeros_like(backs)
    backs = jnp.concatenate([jnp.where(of_image, backs, zero), jnp.where(of_image, zero, backs)])
    for k in range(out_ref.shape[0]):
        out_ref[k] = dot(turned_ref[k], backs, 1, 0).astype(out_ref.dtype)


def layers_kernel(cut, both, mine_ref, theirs_ref, *refs):
    own, parts = cut[0] * 128, cut[1]
    lanes = refs[0].shape[1]
    refs = list(refs)
    for k in range(mine_ref.shape[0]):
        total = mine_ref[k] + theirs_ref[k].astype(wide)
        second = total[:, lanes:own]
        if parts:
            part = total.shape[0] // parts
            extra = total[:part, own:]
            for i in range(1, parts):
                mine = lax.axis_index("blk") % parts == i
                extra = jnp.where(mine, total[i * part : (i + 1) * part, own:], extra)
            second = jnp.concatenate([second, extra])
        found = [total[:, :lanes], second]
        for value in [joined(*found)] if both and k == 1 else found:
            ref = refs.pop(0)
            ref[...] = value.astype(ref.dtype)


def joined(first, second):
    count = first.shape[1] // second.shape[1]
    step = second.shape[0] // count
    return jnp.concatenate([first, jnp.concatenate([second[i * step : (i + 1) * step] for i in range(count)], axis=1)])


def parted(array, share):
    rest = array[share:]
    return array[:share], jnp.concatenate([rest[:, i : i + 128] for i in range(0, array.shape[1], 128)])


def sums_kernel(share, group, own_ref, both_ref, *refs):
    *part_refs, out_ref = refs
    total = own_ref[...] + parted(both_ref[...].astype(wide), share)[group]
    for ref in part_refs:
        total = total + ref[...].astype(wide)
    out_ref[...] = total.astype(low)


def heads_kernel(groups, cut, *refs):
    *block_refs, image_ref, text_ref, all_ref = refs
    (share, width), (_, lanes), (own, parts) = image_ref.shape, block_refs[0].shape, (cut[0] * 128, cut[1])
    for k in range(groups):
        blk = k ^ lax.axis_index("blk")
        start = pl.multiple_of(blk * own, 128)
        first, second = (block_refs[i * groups + k][...].astype(wide) for i in (0, 1))
        all_ref[:, pl.ds(start, lanes)] = first
        all_ref[:, pl.ds(start + lanes, own - lanes)] = second[:share]
        if parts:
            part = share // parts
            row = pl.multiple_of(blk % parts * part, 8)
            column = pl.multiple_of(extra_chunk(cut, groups, blk) * 128, 128)
            all_ref[pl.ds(row, part), pl.ds(column, 128)] = second[share:]
    image_ref[...] = all_ref[:, :width]
    text_ref[...] = all_ref[:, width : 2 * width]


def per_device(images, captions, image_head, text_head):
    groups = lax.axis_size("blk")
    layers = lax.axis_size("layer")
    cores = lax.axis_size("core")
    rows, width = images.shape
    half = groups * rows

    def over(array, axis, by):
        return lax.ppermute(array, axis, [(i, i ^ by) for i in range(lax.axis_size(axis))])

    def over_blk(array):
        return [array] + [over(array, "blk", k) for k in range(1, groups)]

    def over_layers(blocks):
        parts = [over(block, "layer", k) for k, block in reversed(list(enumerate(blocks, 1)))]
        return parts[::-1]

    def over_core(array):
        return over(array, "core", 1)

    share = width // (layers * cores)
    cut = cuts(2 * width // 128, groups, share)
    own, parts = cut[0] * 128, cut[1]
    lanes = own + 128 * (parts > 0)
    columns = max(groups * own, 2 * width)
    first = (share, own - 128 if parts else -(-own // 256) * 128)
    second = (share + share // parts, 128) if parts else (share, own - first[1])
    assert width % 128 == 0 and cores == 2

    block = (rows, width)

    caption_blocks = over_blk(captions)
    image_blocks = [over(images, "layer", k) for k in range(1, layers)]
    image_own, text_own = call(own_kernel, [(block, low)] * 2, images, captions, cost=10)
    caption_blocks[0] = text_own
    outs = [(block, low), ((half, width), low)]
    image_own, near_low = call(text_kernel, outs, image_own, *caption_blocks, text_head, cost=2)
    image_group = over_blk(image_own)
    far_low = over_core(near_low)
    image_low = call(
        rows_kernel,
        [((layers * rows, width), low)],
        *(image_own, *image_blocks, image_head),
        behind=(near_low,),
        cost=10,
    )[0]
    outs = [(block, wide)] + [(block, low)] * (layers - 1) + [((half, width), wide), ((half, width), low)]
    image_total, *image_out, near_part, far_part = call(tile_kernel, outs, image_low, near_low, far_low, cost=1)
    image_out[0] = call(own_kernel, [(block, low)], image_out[0], behind=image_group[1:], cost=6)[0]
    image_parts = over_layers(image_out)
    outs = [(block, wide)] + [(block, low)] * (groups - 1)
    text_total, *text_out = call(half_kernel, outs, near_part, over_core(far_part), cost=1)
    text_parts = [over(block, "blk", k + 1) for k, block in enumerate(text_out)]

    turned = [((count, share, 2 * half), low) for count in (near, layers - near)]
    image_before, text_before, *turned = call(
        functools.partial(ready_kernel, (groups, layers, cores)),
        [(block, wide), (block, wide), *turned, *turned],
        *(image_head, text_head, *image_group, *caption_blocks),
        scratch=[((width, 2 * half), wide)],
        behind=text_out[:1],
        cost=1,
    )
    image_back, text_back, *sends = call(
        functools.partial(backs_kernel, layers, groups, cut),
        [(block, low)] * 2 + [((rows, lanes), low)] * groups,
        *(image_total, image_before, *image_parts, text_total, text_before, *text_parts),
        cost=80,
        scratch=[((rows, columns), low)],
    )
    backs = [sends[0]] + [over(sends[k], "blk", k) for k in range(groups - 1, 0, -1)]
    count = first[1] // 128
    both = second[1] == 128 and second[0] % (8 * count) == 0 and share % 8 == 0
    pair = [(first, low), (second, low)]
    joint = (share + second[0] // count, first[1])
    kernel = functools.partial(terms_kernel, width, groups, cut)
    sums, made = [], backs[:1]
    for i, outs in ((1, pair * (layers - near)), (0, [(first, wide), (second, wide)] + ([(joint, low)] if both else pair))):
        shape = (layers - near if i else near, share, lanes)
        theirs = call(kernel, [(shape, low)], turned[2 + i], *backs, behind=made)[0]
        mine = call(kernel, [(shape, wide)], turned[i], *backs, behind=[theirs])[0]
        made = [theirs]
        sums.append(call(functools.partial(layers_kernel, cut, both and not i), outs, mine, over_core(theirs)))
    terms, (first_own, second_own, *nearest) = sums
    next_layer = [over(block, "layer", 1) for block in nearest]
    first_parts, second_parts = (
        [over(terms[2 * k - 4 + i], "layer", k) for k in range(layers - 1, 1, -1)] for i in (0, 1)
    )
    grad_images, grad_captions, token = call(
        grads_kernel,
        [(block, low), (block, low), ((8, 128), wide)],
        *(image_back, image_head, text_back, text_head),
        behind=[mine],
    )
    if both:
        kernels = [functools.partial(sums_kernel, share, i) for i in (0, 1)]
        next_layer = next_layer * 2
    else:
        kernels = [sum_kernel] * 2
    added = call(add_kernel, [(first, wide)], *first_parts, cost=6)[0]
    first_sum = call(kernels[0], [(first, low)], first_own, next_layer[0], added, cost=50, behind=[token])[0]
    first_sums = over_blk(first_sum)
    second_sum = call(kernels[1], [(second, low)], second_own, next_layer[1], *second_parts, cost=1)[0]
    later_sum = call(own_kernel, [(second, low)], second_sum, behind=first_sums[1:2], cost=1)[0]
    second_sums = [over(second_sum, "blk", k) for k in range(groups - 1, 0, -1) if k != 1][::-1]
    second_sums.insert(1 - 1, over(later_sum, "blk", 1))
    blocks = first_sums + [second_sum] + second_sums
    token = call(token_kernel, [((8, 128), wide)], behind=first_sums[2:], cost=10)[0]
    grad_image_head, grad_text_head = call(
        functools.partial(heads_kernel, groups, cut),
        [((share, width), wide)] * 2,
        *blocks,
        scratch=[((share, columns), wide)],
        behind=[token],
    )
    return (grad_images, grad_captions, grad_image_head, grad_text_head)


def solution(mesh):
    groups, members = mesh.devices.shape
    fine = Mesh(mesh.devices.reshape(groups, members // 2, 2), ("blk", "layer", "core"))
    pairs, share = P(("blk", "layer", "core"), None), P(("layer", "core"), None)
    return jax.shard_map(
        per_device,
        mesh=fine,
        in_specs=(pairs, pairs, P(), P()),
        out_specs=(pairs, pairs, share, share),
        check_vma=False,
    )
```

```python
import functools
import math

import jax
import jax.numpy as jnp
from jax import lax
from jax.experimental import pallas as pl
from jax.experimental.pallas import tpu as pltpu
from jax.sharding import Mesh
from jax.sharding import PartitionSpec as P

logit_scale = 32.0
logit_bias = -3.0
epsilon = 1e-06
low = jnp.bfloat16
near = 2
wide = jnp.float32
cost_unit = 1_000_000_000


def dot(a, b, a_dim, b_dim):
    return lax.dot_general(a, b, (((a_dim,), (b_dim,)), ((), ())), preferred_element_type=wide)


def project(features, weight):
    before = dot(features, weight, 1, 0)
    return (before, normalized(before)[0].astype(low))


def normalized(before):
    inverse = lax.rsqrt(jnp.sum(before * before, axis=1, keepdims=True) + epsilon)
    return (before * inverse, inverse)


def call(kernel, outs, *arrays, cost=1, scratch=(), behind=()):
    specs = [pl.BlockSpec(memory_space=pltpu.VMEM)] * len(arrays)
    count = len(arrays)
    shapes = [shape for shape, _ in (*outs, *scratch)] + [array.shape for array in arrays]
    held = sum(math.prod(shape) * 4 for shape in shapes)

    def body(*refs):
        kernel(*refs[:count], *refs[count + len(behind) :])

    return pl.pallas_call(
        body,
        out_shape=tuple(jax.ShapeDtypeStruct(shape, kind) for shape, kind in outs),
        in_specs=specs + [pl.BlockSpec(memory_space=pl.ANY)] * len(behind),
        out_specs=(pl.BlockSpec(memory_space=pltpu.VMEM),) * len(outs),
        scratch_shapes=[pltpu.VMEM(shape, kind) for shape, kind in scratch],
        compiler_params=pltpu.CompilerParams(vmem_limit_bytes=min(48 * 2**20, 4 * 2**20 + held)),
        cost_estimate=pl.CostEstimate(flops=cost * cost_unit, bytes_accessed=cost * cost_unit, transcendentals=0),
    )(*arrays, *behind)


def ready_kernel(shape, image_head_ref, text_head_ref, *refs):
    groups, layers, cores = shape
    image_refs, text_refs, refs = refs[:groups], refs[groups : 2 * groups], refs[2 * groups :]
    image_before_ref, text_before_ref, *out_refs, turned_ref = refs
    image_before_ref[...] = dot(image_refs[0][...], image_head_ref[...], 1, 0)
    text_before_ref[...] = dot(text_refs[0][...], text_head_ref[...], 1, 0)
    gathered = jnp.concatenate([ref[...].astype(wide) for ref in (*image_refs, *text_refs)])
    turned_ref[...] = gathered.T
    share, layer_pos, core_pos = out_refs[0].shape[1], lax.axis_index("layer"), lax.axis_index("core")
    step = math.gcd(share, 8)
    for k in range(layers):
        for i, core in enumerate((core_pos, 1 - core_pos)):
            first = ((k ^ layer_pos) * cores + core) * share
            rows = turned_ref[pl.ds(pl.multiple_of(first // 8 * 8, 8), -(-share // 8) * 8), :]
            for start in range(step, 8, step):
                rows = jnp.where(first % 8 == start, pltpu.roll(rows, rows.shape[0] - start, 0), rows)
            out_refs[2 * i + (k >= near)][k - near * (k >= near)] = rows[:share].astype(low)


def own_kernel(*refs):
    for k in range(len(refs) // 2):
        refs[len(refs) // 2 + k][...] = refs[k][...]


def text_kernel(image_ref, *refs):
    *in_refs, image_out_ref, low_ref = refs
    rows_kernel(*in_refs, low_ref)
    image_out_ref[...] = image_ref[...]


def rows_kernel(*refs):
    *block_refs, head_ref, low_ref = refs
    low_ref[...] = project(jnp.concatenate([ref[...] for ref in block_refs]), head_ref[...])[1]


def token_kernel(out_ref):
    out_ref[...] = jnp.zeros_like(out_ref)


def half_kernel(near_ref, far_ref, own_ref, *block_refs):
    total = near_ref[...] + far_ref[...].astype(wide)
    rows = own_ref.shape[0]
    own_ref[...] = total[:rows]
    for k, ref in enumerate(block_refs):
        ref[...] = total[(k + 1) * rows : (k + 2) * rows].astype(ref.dtype)


def back_of(own_ref, before_ref, part_refs):
    total = own_ref[...]
    for ref in part_refs:
        total = total + ref[...].astype(wide)
    unit, inverse = normalized(before_ref[...])
    grad_unit = logit_scale * total
    inner_sum = jnp.sum(unit * grad_unit, axis=1, keepdims=True)
    return (inverse * (grad_unit - unit * inner_sum)).astype(low)


def cuts(chunks, groups, share):
    full, rest = divmod(chunks, groups)
    parts = groups // rest if rest and groups % rest == 0 else 0
    if parts and share % (8 * parts) == 0:
        return full, parts
    return full + (rest > 0), 0


def extra_chunk(cut, groups, blk):
    full, parts = cut
    return groups * full + blk // parts


def backs_kernel(layers, groups, cut, *refs):
    image_refs, refs = refs[: layers + 1], refs[layers + 1 :]
    text_refs, refs = refs[: groups + 1], refs[groups + 1 :]
    image_ref, text_ref, *out_refs, all_ref = refs
    width = image_ref.shape[1]
    image_ref[...] = back_of(*image_refs[:2], image_refs[2:])
    text_ref[...] = back_of(*text_refs[:2], text_refs[2:])
    all_ref[:, :width] = image_ref[...]
    all_ref[:, width : 2 * width] = text_ref[...]
    if all_ref.shape[1] > 2 * width:
        all_ref[:, 2 * width :] = jnp.zeros((all_ref.shape[0], all_ref.shape[1] - 2 * width), low)
    own = cut[0] * 128
    for k, ref in enumerate(out_refs):
        blk = k ^ lax.axis_index("blk")
        ref[:, :own] = all_ref[:, pl.ds(pl.multiple_of(blk * own, 128), own)]
        if cut[1]:
            first = pl.multiple_of(extra_chunk(cut, groups, blk) * 128, 128)
            ref[:, own:] = all_ref[:, pl.ds(first, 128)]


def grads_kernel(image_ref, image_head_ref, text_ref, text_head_ref, image_out_ref, text_out_ref, token_ref):
    image_out_ref[...] = dot(image_ref[...], image_head_ref[...], 1, 1).astype(low)
    text_out_ref[...] = dot(text_ref[...], text_head_ref[...], 1, 1).astype(low)
    token_ref[...] = jnp.zeros_like(token_ref)


def add_kernel(*refs):
    *part_refs, out_ref = refs
    total = part_refs[0][...].astype(wide)
    for ref in part_refs[1:]:
        total = total + ref[...].astype(wide)
    out_ref[...] = total


def sum_kernel(own_ref, *refs):
    *part_refs, out_ref = refs
    total = own_ref[...]
    for ref in part_refs:
        total = total + ref[...].astype(wide)
    out_ref[...] = total.astype(low)


def tile_kernel(images_ref, near_ref, far_ref, own_ref, *refs):
    *part_refs, near_part_ref, far_part_ref = refs
    images = images_ref[...]
    rows = own_ref.shape[0]
    near, far = near_ref[...], far_ref[...]
    logits = logit_scale * dot(images, near, 1, 1) + logit_bias
    row = lax.broadcasted_iota(jnp.int32, logits.shape, 0)
    column = lax.broadcasted_iota(jnp.int32, logits.shape, 1)
    sign = jnp.where((row == column) & (row < rows), wide(1.0), wide(-1.0))
    near_weight = (-sign * jax.nn.sigmoid(-sign * logits)).astype(low)
    far_weight = jax.nn.sigmoid(logit_scale * dot(images, far, 1, 1) + logit_bias).astype(low)
    far_part_ref[...] = dot(far_weight, images, 0, 0).astype(low)
    near_part_ref[...] = dot(near_weight, images, 0, 0)
    parts = dot(near_weight, near, 1, 0) + dot(far_weight, far, 1, 0)
    own_ref[...] = parts[:rows]
    for k, ref in enumerate(part_refs):
        ref[...] = parts[(k + 1) * rows : (k + 2) * rows].astype(low)


def terms_kernel(width, groups, cut, turned_ref, *refs):
    *back_refs, out_ref = refs
    backs = jnp.concatenate([ref[...] for ref in back_refs[:1] + back_refs[:0:-1]])
    blk, own = lax.axis_index("blk"), cut[0] * 128
    lane = lax.broadcasted_iota(jnp.int32, backs.shape, 1)
    column = lane + blk * own
    if cut[1]:
        column = jnp.where(lane < own, column, lane - own + extra_chunk(cut, groups, blk) * 128)
    of_image = column < width
    zero = jnp.zeros_like(backs)
    backs = jnp.concatenate([jnp.where(of_image, backs, zero), jnp.where(of_image, zero, backs)])
    for k in range(out_ref.shape[0]):
        out_ref[k] = dot(turned_ref[k], backs, 1, 0).astype(out_ref.dtype)


def layers_kernel(cut, both, mine_ref, theirs_ref, *refs):
    own, parts = cut[0] * 128, cut[1]
    lanes = refs[0].shape[1]
    refs = list(refs)
    for k in range(mine_ref.shape[0]):
        total = mine_ref[k] + theirs_ref[k].astype(wide)
        second = total[:, lanes:own]
        if parts:
            part = total.shape[0] // parts
            extra = total[:part, own:]
            for i in range(1, parts):
                mine = lax.axis_index("blk") % parts == i
                extra = jnp.where(mine, total[i * part : (i + 1) * part, own:], extra)
            second = jnp.concatenate([second, extra])
        found = [total[:, :lanes], second]
        for value in [joined(*found)] if both and k == 1 else found:
            ref = refs.pop(0)
            ref[...] = value.astype(ref.dtype)


def joined(first, second):
    count = first.shape[1] // second.shape[1]
    step = second.shape[0] // count
    return jnp.concatenate([first, jnp.concatenate([second[i * step : (i + 1) * step] for i in range(count)], axis=1)])


def parted(array, share):
    rest = array[share:]
    return array[:share], jnp.concatenate([rest[:, i : i + 128] for i in range(0, array.shape[1], 128)])


def sums_kernel(share, group, own_ref, both_ref, *refs):
    *part_refs, out_ref = refs
    total = own_ref[...] + parted(both_ref[...].astype(wide), share)[group]
    for ref in part_refs:
        total = total + ref[...].astype(wide)
    out_ref[...] = total.astype(low)


def heads_kernel(groups, cut, *refs):
    *block_refs, image_ref, text_ref, all_ref = refs
    (share, width), (_, lanes), (own, parts) = image_ref.shape, block_refs[0].shape, (cut[0] * 128, cut[1])
    for k in range(groups):
        blk = k ^ lax.axis_index("blk")
        start = pl.multiple_of(blk * own, 128)
        first, second = (block_refs[i * groups + k][...].astype(wide) for i in (0, 1))
        all_ref[:, pl.ds(start, lanes)] = first
        all_ref[:, pl.ds(start + lanes, own - lanes)] = second[:share]
        if parts:
            part = share // parts
            row = pl.multiple_of(blk % parts * part, 8)
            column = pl.multiple_of(extra_chunk(cut, groups, blk) * 128, 128)
            all_ref[pl.ds(row, part), pl.ds(column, 128)] = second[share:]
    image_ref[...] = all_ref[:, :width]
    text_ref[...] = all_ref[:, width : 2 * width]


def per_device(images, captions, image_head, text_head):
    groups = lax.axis_size("blk")
    layers = lax.axis_size("layer")
    cores = lax.axis_size("core")
    rows, width = images.shape
    half = groups * rows

    def over(array, axis, by):
        return lax.ppermute(array, axis, [(i, i ^ by) for i in range(lax.axis_size(axis))])

    def over_blk(array):
        return [array] + [over(array, "blk", k) for k in range(1, groups)]

    def over_layers(blocks):
        parts = [over(block, "layer", k) for k, block in reversed(list(enumerate(blocks, 1)))]
        return parts[::-1]

    def over_core(array):
        return over(array, "core", 1)

    share = width // (layers * cores)
    cut = cuts(2 * width // 128, groups, share)
    own, parts = cut[0] * 128, cut[1]
    lanes = own + 128 * (parts > 0)
    columns = max(groups * own, 2 * width)
    first = (share, own - 128 if parts else -(-own // 256) * 128)
    second = (share + share // parts, 128) if parts else (share, own - first[1])
    assert width % 128 == 0 and cores == 2

    block = (rows, width)

    caption_blocks = over_blk(captions)
    image_blocks = [over(images, "layer", k) for k in range(1, layers)]
    image_own, text_own = call(own_kernel, [(block, low)] * 2, images, captions, cost=10)
    caption_blocks[0] = text_own
    outs = [(block, low), ((half, width), low)]
    image_own, near_low = call(text_kernel, outs, image_own, *caption_blocks, text_head, cost=2)
    image_group = over_blk(image_own)
    far_low = over_core(near_low)
    image_low = call(
        rows_kernel,
        [((layers * rows, width), low)],
        *(image_own, *image_blocks, image_head),
        behind=(near_low,),
        cost=10,
    )[0]
    outs = [(block, wide)] + [(block, low)] * (layers - 1) + [((half, width), wide), ((half, width), low)]
    image_total, *image_out, near_part, far_part = call(tile_kernel, outs, image_low, near_low, far_low, cost=1)
    image_out[0] = call(own_kernel, [(block, low)], image_out[0], behind=image_group[1:], cost=6)[0]
    image_parts = over_layers(image_out)
    outs = [(block, wide)] + [(block, low)] * (groups - 1)
    text_total, *text_out = call(half_kernel, outs, near_part, over_core(far_part), cost=1)
    text_parts = [over(block, "blk", k + 1) for k, block in enumerate(text_out)]

    turned = [((count, share, 2 * half), low) for count in (near, layers - near)]
    image_before, text_before, *turned = call(
        functools.partial(ready_kernel, (groups, layers, cores)),
        [(block, wide), (block, wide), *turned, *turned],
        *(image_head, text_head, *image_group, *caption_blocks),
        scratch=[((width, 2 * half), wide)],
        behind=text_out[:1],
        cost=1,
    )
    image_back, text_back, *sends = call(
        functools.partial(backs_kernel, layers, groups, cut),
        [(block, low)] * 2 + [((rows, lanes), low)] * groups,
        *(image_total, image_before, *image_parts, text_total, text_before, *text_parts),
        cost=80,
        scratch=[((rows, columns), low)],
    )
    backs = [sends[0]] + [over(sends[k], "blk", k) for k in range(groups - 1, 0, -1)]
    grad_images, grad_captions, token = call(
        grads_kernel,
        [(block, low), (block, low), ((8, 128), wide)],
        *(image_back, image_head, text_back, text_head),
        behind=sends[:1],
    )
    count = first[1] // 128
    both = second[1] == 128 and second[0] % (8 * count) == 0 and share % 8 == 0
    pair = [(first, low), (second, low)]
    joint = (share + second[0] // count, first[1])
    kernel = functools.partial(terms_kernel, width, groups, cut)
    sums, made = [], [token]
    farther = [part for k in range(near, layers) for part in ((first, low), (second, wide if both and k % 2 == 0 else low))]
    for i, outs in ((1, farther), (0, [(first, wide), (second, wide)] + ([(joint, low)] if both else pair))):
        shape = (layers - near if i else near, share, lanes)
        theirs = call(kernel, [(shape, low)], turned[2 + i], *backs, behind=made)[0]
        mine = call(kernel, [(shape, wide)], turned[i], *backs, behind=[theirs])[0]
        made = [theirs]
        sums.append(call(functools.partial(layers_kernel, cut, both and not i), outs, mine, over_core(theirs)))
    terms, (first_own, second_own, *nearest) = sums
    next_layer = [over(block, "layer", 1) for block in nearest]
    first_parts = [over(part, "layer", k) for k, part in reversed(list(enumerate(terms[::2], near)))]
    second_parts = []
    if both:
        for k in range(near, layers, 2):
            passed = over(terms[2 * (k + 1 - near) + 1], "layer", 1)
            passed = call(sum_kernel, [(second, low)], terms[2 * (k - near) + 1], passed, cost=1)[0]
            second_parts.append(over(passed, "layer", k))
    else:
        second_parts = [over(part, "layer", k) for k, part in reversed(list(enumerate(terms[1::2], near)))]
    if both:
        kernels = [functools.partial(sums_kernel, share, i) for i in (0, 1)]
        next_layer = next_layer * 2
    else:
        kernels = [sum_kernel] * 2
    added = call(add_kernel, [(first, wide)], *first_parts, cost=6)[0]
    first_sum = call(kernels[0], [(first, low)], first_own, next_layer[0], added, cost=50)[0]
    first_sums = over_blk(first_sum)
    second_sum = call(kernels[1], [(second, low)], second_own, next_layer[1], *second_parts, cost=1)[0]
    later_sum = call(own_kernel, [(second, low)], second_sum, behind=first_sums[1:2], cost=1)[0]
    second_sums = [over(second_sum, "blk", k) for k in range(groups - 1, 0, -1) if k != 1][::-1]
    second_sums.insert(1 - 1, over(later_sum, "blk", 1))
    blocks = first_sums + [second_sum] + second_sums
    token = call(token_kernel, [((8, 128), wide)], behind=first_sums[2:], cost=10)[0]
    grad_image_head, grad_text_head = call(
        functools.partial(heads_kernel, groups, cut),
        [((share, width), wide)] * 2,
        *blocks,
        scratch=[((share, columns), wide)],
        behind=[token],
    )
    return (grad_images, grad_captions, grad_image_head, grad_text_head)


def solution(mesh):
    groups, members = mesh.devices.shape
    fine = Mesh(mesh.devices.reshape(groups, members // 2, 2), ("blk", "layer", "core"))
    pairs, share = P(("blk", "layer", "core"), None), P(("layer", "core"), None)
    return jax.shard_map(
        per_device,
        mesh=fine,
        in_specs=(pairs, pairs, P(), P()),
        out_specs=(pairs, pairs, share, share),
        check_vma=False,
    )
```

```python
import functools
import math

import jax
import jax.numpy as jnp
from jax import lax
from jax.experimental import pallas as pl
from jax.experimental.pallas import tpu as pltpu
from jax.sharding import Mesh
from jax.sharding import PartitionSpec as P

logit_scale = 32.0
logit_bias = -3.0
epsilon = 1e-06
low = jnp.bfloat16
near = 2
wide = jnp.float32
cost_unit = 1_000_000_000


def dot(a, b, a_dim, b_dim):
    return lax.dot_general(a, b, (((a_dim,), (b_dim,)), ((), ())), preferred_element_type=wide)


def project(features, weight):
    before = dot(features, weight, 1, 0)
    return (before, normalized(before)[0].astype(low))


def normalized(before):
    inverse = lax.rsqrt(jnp.sum(before * before, axis=1, keepdims=True) + epsilon)
    return (before * inverse, inverse)


def call(kernel, outs, *arrays, cost=1, scratch=(), behind=(), copies=0):
    specs = [pl.BlockSpec(memory_space=pltpu.VMEM)] * len(arrays)
    count = len(arrays)
    shapes = [shape for shape, _ in (*outs, *scratch)] + [array.shape for array in arrays]
    held = sum(math.prod(shape) * 4 for shape in shapes)

    def body(*refs):
        kernel(*refs[:count], *refs[count + len(behind) :])

    return pl.pallas_call(
        body,
        out_shape=tuple(jax.ShapeDtypeStruct(shape, kind) for shape, kind in outs),
        in_specs=specs + [pl.BlockSpec(memory_space=pl.ANY)] * len(behind),
        out_specs=(pl.BlockSpec(memory_space=pl.ANY if copies else pltpu.VMEM),) * len(outs),
        scratch_shapes=[pltpu.VMEM(shape, kind) for shape, kind in scratch]
        + [pltpu.SemaphoreType.DMA((copies,))] * (copies > 0),
        compiler_params=pltpu.CompilerParams(vmem_limit_bytes=min(48 * 2**20, 4 * 2**20 + held)),
        cost_estimate=pl.CostEstimate(flops=cost * cost_unit, bytes_accessed=cost * cost_unit, transcendentals=0),
    )(*arrays, *behind)


def ready_kernel(shape, image_head_ref, text_head_ref, *refs):
    groups, layers, cores = shape
    image_refs, text_refs, refs = refs[:groups], refs[groups : 2 * groups], refs[2 * groups :]
    image_before_ref, text_before_ref, *out_refs, turned_ref = refs
    image_before_ref[...] = dot(image_refs[0][...], image_head_ref[...], 1, 0)
    text_before_ref[...] = dot(text_refs[0][...], text_head_ref[...], 1, 0)
    gathered = jnp.concatenate([ref[...].astype(wide) for ref in (*image_refs, *text_refs)])
    turned_ref[...] = gathered.T
    share, layer_pos, core_pos = out_refs[0].shape[1], lax.axis_index("layer"), lax.axis_index("core")
    step = math.gcd(share, 8)
    for k in range(layers):
        for i, core in enumerate((core_pos, 1 - core_pos)):
            first = ((k ^ layer_pos) * cores + core) * share
            rows = turned_ref[pl.ds(pl.multiple_of(first // 8 * 8, 8), -(-share // 8) * 8), :]
            for start in range(step, 8, step):
                rows = jnp.where(first % 8 == start, pltpu.roll(rows, rows.shape[0] - start, 0), rows)
            out_refs[2 * i + (k >= near)][k - near * (k >= near)] = rows[:share].astype(low)


def own_kernel(*refs):
    for k in range(len(refs) // 2):
        refs[len(refs) // 2 + k][...] = refs[k][...]


def text_kernel(image_ref, *refs):
    *in_refs, image_out_ref, low_ref = refs
    rows_kernel(*in_refs, low_ref)
    image_out_ref[...] = image_ref[...]


def rows_kernel(*refs):
    *block_refs, head_ref, low_ref = refs
    low_ref[...] = project(jnp.concatenate([ref[...] for ref in block_refs]), head_ref[...])[1]


def token_kernel(out_ref):
    out_ref[...] = jnp.zeros_like(out_ref)


def half_kernel(near_ref, far_ref, own_ref, *block_refs):
    total = near_ref[...] + far_ref[...].astype(wide)
    rows = own_ref.shape[0]
    own_ref[...] = total[:rows]
    for k, ref in enumerate(block_refs):
        ref[...] = total[(k + 1) * rows : (k + 2) * rows].astype(ref.dtype)


def back_of(own_ref, before_ref, part_refs):
    total = own_ref[...]
    for ref in part_refs:
        total = total + ref[...].astype(wide)
    unit, inverse = normalized(before_ref[...])
    grad_unit = logit_scale * total
    inner_sum = jnp.sum(unit * grad_unit, axis=1, keepdims=True)
    return (inverse * (grad_unit - unit * inner_sum)).astype(low)


def cuts(chunks, groups, share):
    full, rest = divmod(chunks, groups)
    parts = groups // rest if rest and groups % rest == 0 else 0
    if parts and share % (8 * parts) == 0:
        return full, parts
    return full + (rest > 0), 0


def extra_chunk(cut, groups, blk):
    full, parts = cut
    return groups * full + blk // parts


def backs_kernel(layers, groups, cut, *refs):
    image_refs, refs = refs[: layers + 1], refs[layers + 1 :]
    text_refs, refs = refs[: groups + 1], refs[groups + 1 :]
    image_ref, text_ref, *out_refs, all_ref = refs
    width = image_ref.shape[1]
    image_ref[...] = back_of(*image_refs[:2], image_refs[2:])
    text_ref[...] = back_of(*text_refs[:2], text_refs[2:])
    all_ref[:, :width] = image_ref[...]
    all_ref[:, width : 2 * width] = text_ref[...]
    if all_ref.shape[1] > 2 * width:
        all_ref[:, 2 * width :] = jnp.zeros((all_ref.shape[0], all_ref.shape[1] - 2 * width), low)
    own = cut[0] * 128
    for k, ref in enumerate(out_refs):
        blk = k ^ lax.axis_index("blk")
        ref[:, :own] = all_ref[:, pl.ds(pl.multiple_of(blk * own, 128), own)]
        if cut[1]:
            first = pl.multiple_of(extra_chunk(cut, groups, blk) * 128, 128)
            ref[:, own:] = all_ref[:, pl.ds(first, 128)]


def grads_kernel(image_ref, image_head_ref, text_ref, text_head_ref, image_out_ref, text_out_ref, token_ref):
    image_out_ref[...] = dot(image_ref[...], image_head_ref[...], 1, 1).astype(low)
    text_out_ref[...] = dot(text_ref[...], text_head_ref[...], 1, 1).astype(low)
    token_ref[...] = jnp.zeros_like(token_ref)


def add_kernel(*refs):
    *part_refs, out_ref = refs
    total = part_refs[0][...].astype(wide)
    for ref in part_refs[1:]:
        total = total + ref[...].astype(wide)
    out_ref[...] = total


def sum_kernel(own_ref, *refs):
    *part_refs, out_ref = refs
    total = own_ref[...]
    for ref in part_refs:
        total = total + ref[...].astype(wide)
    out_ref[...] = total.astype(low)


def tile_kernel(images_ref, near_ref, far_ref, own_ref, *refs):
    *part_refs, near_part_ref, far_part_ref = refs
    images = images_ref[...]
    rows = own_ref.shape[0]
    near, far = near_ref[...], far_ref[...]
    logits = logit_scale * dot(images, near, 1, 1) + logit_bias
    row = lax.broadcasted_iota(jnp.int32, logits.shape, 0)
    column = lax.broadcasted_iota(jnp.int32, logits.shape, 1)
    sign = jnp.where((row == column) & (row < rows), wide(1.0), wide(-1.0))
    near_weight = (-sign * jax.nn.sigmoid(-sign * logits)).astype(low)
    far_weight = jax.nn.sigmoid(logit_scale * dot(images, far, 1, 1) + logit_bias).astype(low)
    far_part_ref[...] = dot(far_weight, images, 0, 0).astype(low)
    near_part_ref[...] = dot(near_weight, images, 0, 0)
    parts = dot(near_weight, near, 1, 0) + dot(far_weight, far, 1, 0)
    own_ref[...] = parts[:rows]
    for k, ref in enumerate(part_refs):
        ref[...] = parts[(k + 1) * rows : (k + 2) * rows].astype(low)


def terms_kernel(width, groups, cut, turned_ref, *refs):
    *back_refs, out_ref = refs
    backs = jnp.concatenate([ref[...] for ref in back_refs[:1] + back_refs[:0:-1]])
    blk, own = lax.axis_index("blk"), cut[0] * 128
    lane = lax.broadcasted_iota(jnp.int32, backs.shape, 1)
    column = lane + blk * own
    if cut[1]:
        column = jnp.where(lane < own, column, lane - own + extra_chunk(cut, groups, blk) * 128)
    of_image = column < width
    zero = jnp.zeros_like(backs)
    backs = jnp.concatenate([jnp.where(of_image, backs, zero), jnp.where(of_image, zero, backs)])
    for k in range(out_ref.shape[0]):
        out_ref[k] = dot(turned_ref[k], backs, 1, 0).astype(out_ref.dtype)


def layers_kernel(cut, both, mine_ref, theirs_ref, *refs):
    own, parts = cut[0] * 128, cut[1]
    lanes = refs[0].shape[1]
    refs = list(refs)
    for k in range(mine_ref.shape[0]):
        total = mine_ref[k] + theirs_ref[k].astype(wide)
        second = total[:, lanes:own]
        if parts:
            part = total.shape[0] // parts
            extra = total[:part, own:]
            for i in range(1, parts):
                mine = lax.axis_index("blk") % parts == i
                extra = jnp.where(mine, total[i * part : (i + 1) * part, own:], extra)
            second = jnp.concatenate([second, extra])
        found = [total[:, :lanes], second]
        for value in [joined(*found)] if both and k == 1 else found:
            ref = refs.pop(0)
            ref[...] = value.astype(ref.dtype)


def joined(first, second):
    count = first.shape[1] // second.shape[1]
    step = second.shape[0] // count
    return jnp.concatenate([first, jnp.concatenate([second[i * step : (i + 1) * step] for i in range(count)], axis=1)])


def parted(array, share):
    rest = array[share:]
    return array[:share], jnp.concatenate([rest[:, i : i + 128] for i in range(0, array.shape[1], 128)])


def sums_kernel(share, group, own_ref, both_ref, *refs):
    *part_refs, out_ref = refs
    total = own_ref[...] + parted(both_ref[...].astype(wide), share)[group]
    for ref in part_refs:
        total = total + ref[...].astype(wide)
    out_ref[...] = total.astype(low)


def heads_kernel(groups, cut, *refs):
    *block_refs, image_ref, text_ref, all_ref, sems = refs
    (share, width), (_, lanes), (own, parts) = image_ref.shape, block_refs[0].shape, (cut[0] * 128, cut[1])
    steps = parts or 1
    part = share // steps
    copies = []
    for step in range(steps):
        at = slice(step * part, (step + 1) * part)
        for k in range(groups):
            blk = k ^ lax.axis_index("blk")
            start = pl.multiple_of(blk * own, 128)
            first, second = (block_refs[i * groups + k][...].astype(wide) for i in (0, 1))
            all_ref[at, pl.ds(start, lanes)] = first[at]
            all_ref[at, pl.ds(start + lanes, own - lanes)] = second[at]
            if parts:
                column = pl.multiple_of(extra_chunk(cut, groups, blk) * 128, 128)

                @pl.when(blk % parts == step)
                def _():
                    all_ref[at, pl.ds(column, 128)] = second[share:]

        for i, ref in enumerate((image_ref, text_ref)):
            copies.append(
                pltpu.make_async_copy(all_ref.at[at, i * width : (i + 1) * width], ref.at[at], sems.at[len(copies)])
            )
            copies[-1].start()
    for copy in copies:
        copy.wait()


def per_device(images, captions, image_head, text_head):
    groups = lax.axis_size("blk")
    layers = lax.axis_size("layer")
    cores = lax.axis_size("core")
    rows, width = images.shape
    half = groups * rows

    def over(array, axis, by):
        return lax.ppermute(array, axis, [(i, i ^ by) for i in range(lax.axis_size(axis))])

    def over_blk(array):
        return [array] + [over(array, "blk", k) for k in range(1, groups)]

    def over_layers(blocks):
        parts = [over(block, "layer", k) for k, block in reversed(list(enumerate(blocks, 1)))]
        return parts[::-1]

    def over_core(array):
        return over(array, "core", 1)

    share = width // (layers * cores)
    cut = cuts(2 * width // 128, groups, share)
    own, parts = cut[0] * 128, cut[1]
    lanes = own + 128 * (parts > 0)
    columns = max(groups * own, 2 * width)
    first = (share, own - 128 if parts else -(-own // 256) * 128)
    second = (share + share // parts, 128) if parts else (share, own - first[1])
    assert width % 128 == 0 and cores == 2

    block = (rows, width)

    caption_blocks = over_blk(captions)
    image_blocks = [over(images, "layer", k) for k in range(1, layers)]
    image_own, text_own = call(own_kernel, [(block, low)] * 2, images, captions, cost=10)
    caption_blocks[0] = text_own
    outs = [(block, low), ((half, width), low)]
    image_own, near_low = call(text_kernel, outs, image_own, *caption_blocks, text_head, cost=2)
    image_group = over_blk(image_own)
    far_low = over_core(near_low)
    image_low = call(
        rows_kernel,
        [((layers * rows, width), low)],
        *(image_own, *image_blocks, image_head),
        behind=(near_low,),
        cost=10,
    )[0]
    outs = [(block, wide)] + [(block, low)] * (layers - 1) + [((half, width), wide), ((half, width), low)]
    image_total, *image_out, near_part, far_part = call(tile_kernel, outs, image_low, near_low, far_low, cost=1)
    image_out[0] = call(own_kernel, [(block, low)], image_out[0], behind=image_group[1:], cost=6)[0]
    image_parts = over_layers(image_out)
    outs = [(block, wide)] + [(block, low)] * (groups - 1)
    text_total, *text_out = call(half_kernel, outs, near_part, over_core(far_part), cost=1)
    text_parts = [over(block, "blk", k + 1) for k, block in enumerate(text_out)]

    turned = [((count, share, 2 * half), low) for count in (near, layers - near)]
    image_before, text_before, *turned = call(
        functools.partial(ready_kernel, (groups, layers, cores)),
        [(block, wide), (block, wide), *turned, *turned],
        *(image_head, text_head, *image_group, *caption_blocks),
        scratch=[((width, 2 * half), wide)],
        behind=text_out[:1],
        cost=1,
    )
    image_back, text_back, *sends = call(
        functools.partial(backs_kernel, layers, groups, cut),
        [(block, low)] * 2 + [((rows, lanes), low)] * groups,
        *(image_total, image_before, *image_parts, text_total, text_before, *text_parts),
        cost=80,
        scratch=[((rows, columns), low)],
    )
    backs = [sends[0]] + [over(sends[k], "blk", k) for k in range(groups - 1, 0, -1)]
    grad_images, grad_captions, token = call(
        grads_kernel,
        [(block, low), (block, low), ((8, 128), wide)],
        *(image_back, image_head, text_back, text_head),
        behind=sends[:1],
    )
    count = first[1] // 128
    both = second[1] == 128 and second[0] % (8 * count) == 0 and share % 8 == 0
    pair = [(first, low), (second, low)]
    joint = (share + second[0] // count, first[1])
    kernel = functools.partial(terms_kernel, width, groups, cut)
    sums, made = [], [token]
    farther = [part for k in range(near, layers) for part in ((first, low), (second, wide if both and k % 2 == 0 else low))]
    for i, outs in ((1, farther), (0, [(first, wide), (second, wide)] + ([(joint, low)] if both else pair))):
        shape = (layers - near if i else near, share, lanes)
        theirs = call(kernel, [(shape, low)], turned[2 + i], *backs, behind=made)[0]
        mine = call(kernel, [(shape, wide)], turned[i], *backs, behind=[theirs, *sums[0][:1]] if sums else [theirs])[0]
        made = [theirs]
        sums.append(call(functools.partial(layers_kernel, cut, both and not i), outs, mine, over_core(theirs)))
    terms, (first_own, second_own, *nearest) = sums
    next_layer = [over(block, "layer", 1) for block in nearest]
    first_parts = [over(part, "layer", k) for k, part in reversed(list(enumerate(terms[::2], near)))]
    second_parts = []
    if both:
        for k in range(near, layers, 2):
            passed = over(terms[2 * (k + 1 - near) + 1], "layer", 1)
            passed = call(sum_kernel, [(second, low)], terms[2 * (k - near) + 1], passed, cost=1)[0]
            second_parts.append(over(passed, "layer", k))
    else:
        second_parts = [over(part, "layer", k) for k, part in reversed(list(enumerate(terms[1::2], near)))]
    if both:
        kernels = [functools.partial(sums_kernel, share, i) for i in (0, 1)]
        next_layer = next_layer * 2
    else:
        kernels = [sum_kernel] * 2
    added = call(add_kernel, [(first, wide)], *first_parts, cost=6)[0]
    first_sum = call(kernels[0], [(first, low)], first_own, next_layer[0], added, cost=50)[0]
    first_sums = over_blk(first_sum)
    second_sum = call(kernels[1], [(second, low)], second_own, next_layer[1], *second_parts, cost=1)[0]
    later_sum = call(own_kernel, [(second, low)], second_sum, behind=first_sums[1:2], cost=1)[0]
    second_sums = [over(second_sum, "blk", k) for k in range(groups - 1, 0, -1) if k != 1][::-1]
    second_sums.insert(1 - 1, over(later_sum, "blk", 1))
    blocks = first_sums + [second_sum] + second_sums
    token = call(token_kernel, [((8, 128), wide)], behind=first_sums[2:], cost=10)[0]
    grad_image_head, grad_text_head = call(
        functools.partial(heads_kernel, groups, cut),
        [((share, width), wide)] * 2,
        *blocks,
        scratch=[((share, columns), wide)],
        copies=2 * max(parts, 1),
        behind=[token],
    )
    return (grad_images, grad_captions, grad_image_head, grad_text_head)


def solution(mesh):
    groups, members = mesh.devices.shape
    fine = Mesh(mesh.devices.reshape(groups, members // 2, 2), ("blk", "layer", "core"))
    pairs, share = P(("blk", "layer", "core"), None), P(("layer", "core"), None)
    return jax.shard_map(
        per_device,
        mesh=fine,
        in_specs=(pairs, pairs, P(), P()),
        out_specs=(pairs, pairs, share, share),
        check_vma=False,
    )
```
